32 devices in a mesh: gx: 4 (over z), gy: 2 (over core), gz: 4 (over y, x).
Axes of the slice: x: 2, y: 2, z: 4, core: 2. Of those that a mesh axis runs over, the one named last changes fastest.
Arguments:
- noise: float32 [32, 64, 512], P('gx', 'gy', 'gz'), may hold values from -6 to 6
- kappa_sq: float32 [32, 64, 512], P('gx', 'gy', 'gz'), may hold values from 0.25 to 2
- cuts: int32 [6], replicated, may hold values from 0 to 24, as said below
- pressure_init: float32 [40, 64, 512], P('gx', 'gy', 'gz'), may hold values from -6 to 6
- source: float32 [40, 64, 512], P('gx', 'gy', 'gz'), may hold values from -24 to 24
Outputs:
- field: float32 [32, 64, 512], P('gx', 'gy', 'gz')
- pressure: float32 [40, 64, 512], P('gx', 'gy', 'gz')
The draws below stay inside these ranges and needn't reach their ends.
Inputs may be any that keep to these rules, and one draw needn't show every extreme that they name: cuts[0] lies within 2 of 4; cuts[1] = 0 and cuts[5] = 24; cuts[i+1] lies within 2 of i * 6; in every draw some flow tile holds exactly 10 inset planes.
All inputs are finite; a program needn't handle non-finite values.
Results may differ from the reference program's by a relative error of at most 0.00002.
Values sent between devices are 32-bit elements; how exact they have to be, the bound alone decides.
A program may use at most 64 MiB of HBM per device.

```python
import jax
import jax.numpy as jnp
from jax import lax

SWEEPS = 8
JACOBI = 8
NX = 32
NY = 64
NZ = 512
NX_IN = 24
FLOW_MEAN = 6
JITTER = 2
FLOW_MOST = 10
N_GX = 4


def draw_cuts(key, part):
    first_key, second_key, third_key = jax.random.split(jax.random.fold_in(key, 17), 3)
    inner = jax.random.randint(first_key, (N_GX - 1,), -JITTER, JITTER + 1)
    where_most = jax.random.randint(second_key, (), 0, N_GX - 2)
    inner = inner.at[where_most].set(-JITTER)
    inner = inner.at[where_most + 1].set(JITTER)
    middle = jnp.arange(1, N_GX, dtype=jnp.int32) * FLOW_MEAN + inner
    start = jax.random.randint(third_key, (1,), NX // 8 - JITTER, NX // 8 + JITTER + 1)
    return jnp.concatenate([start.astype(jnp.int32), jnp.zeros((1,), jnp.int32), middle.astype(jnp.int32), jnp.full((1,), NX_IN, jnp.int32)])


def level_of(stream_key, shape, shards, least, largest):
    def one(axis_at, blocks):
        heights = jax.random.uniform(jax.random.fold_in(jax.random.fold_in(stream_key, 6), axis_at), (blocks,), jnp.float32, least / len(shards), largest / len(shards))
        return jnp.repeat(jnp.exp(heights), shape[axis_at] // blocks).reshape((-1,) + (1,) * (len(shape) - axis_at - 1))

    level = one(*shards[0])
    for cut in shards[1:]:
        level = level * one(*cut)
    return level


def normal_values(stream_key, shape, width, most, cuts=(), held_as=jnp.bfloat16):
    values = width * jax.random.normal(stream_key, shape, jnp.float32)
    if cuts:
        values = values * level_of(stream_key, shape, cuts, -0.22, 0.18)
    return jnp.clip(values, -most, most).astype(held_as)


def setup_inputs(seed: int = 0) -> dict:
    key_list = jax.random.split(jax.random.key(seed), 6)
    noise = normal_values(key_list[0], (NX, NY, NZ), 1.0, 6.0, ((0, 4), (1, 2), (2, 4)), jnp.float32)
    kappa_sq = jnp.clip(0.25 + 1.75 * jax.random.uniform(key_list[1], (NX, NY, NZ), jnp.float32) ** level_of(key_list[1], (NX, NY, NZ), ((0, 4), (1, 2), (2, 4)), -0.2, 0.2), 0.25, 2.0)
    cuts = draw_cuts(jax.random.fold_in(key_list[5], 71), 0)
    pressure_init = normal_values(key_list[3], (N_GX * FLOW_MOST, NY, NZ), 1.0, 6.0, ((0, 4), (1, 2), (2, 4)), jnp.float32)
    source = normal_values(key_list[4], (N_GX * FLOW_MOST, NY, NZ), 4.0, 24.0, ((0, 4), (1, 2), (2, 4)), jnp.float32)
    return dict(noise=noise, kappa_sq=kappa_sq, cuts=cuts, pressure_init=pressure_init, source=source)


THETA = 7.125
DELTA = 6.875
LOG_GAIN = 2.0


def sweep_weights(count):
    ratio_base = THETA / DELTA
    ratio_now = 1.0 / ratio_base
    weights = []
    for index in range(count):
        ratio_next = 1.0 / (2.0 * ratio_base - ratio_now)
        weights.append((ratio_next * ratio_now, 2.0 * ratio_next / DELTA))
        ratio_now = ratio_next
    return weights


def apply_matern(values, kappa_sq):
    padded = jnp.pad(values, 1)
    beside = padded[2:, 1:-1, 1:-1] + padded[:-2, 1:-1, 1:-1]
    beside = beside + padded[1:-1, 2:, 1:-1] + padded[1:-1, :-2, 1:-1]
    beside = beside + padded[1:-1, 1:-1, 2:] + padded[1:-1, 1:-1, :-2]
    return (kappa_sq + 6.0) * values - beside


def six_sides(padded):
    return (padded[:-2, 1:-1, 1:-1], padded[2:, 1:-1, 1:-1],
            padded[1:-1, :-2, 1:-1], padded[1:-1, 2:, 1:-1],
            padded[1:-1, 1:-1, :-2], padded[1:-1, 1:-1, 2:])


def harmonic(own, other):
    return 2.0 * own * other / (own + other)


def reference(noise, kappa_sq, cuts, pressure_init, source):
    field = jnp.zeros_like(noise)
    resid = noise
    direction = noise / THETA
    for weight in sweep_weights(SWEEPS):
        field = field + direction
        resid = resid - apply_matern(direction, kappa_sq)
        direction = weight[0] * direction + weight[1] * resid
    bounds = cuts[1:]
    inner = lax.dynamic_slice_in_dim(field, cuts[0].astype(jnp.int32), NX_IN, 0)
    perm = jnp.exp(LOG_GAIN * inner)
    planes = jnp.arange(NX_IN, dtype=jnp.int32)
    tiles = jnp.sum((planes[:, None] >= bounds[None, 1:N_GX]).astype(jnp.int32), axis=1)
    rows = (tiles * FLOW_MOST + planes - bounds[tiles]).astype(jnp.int32)
    pressure = pressure_init[rows]
    charge = source[rows]
    perm_sides = six_sides(jnp.pad(perm, 1, mode="edge"))
    coupling = [harmonic(perm, other) for other in perm_sides]
    total = coupling[0] + coupling[1] + coupling[2] + coupling[3] + coupling[4] + coupling[5]
    for sweep in range(JACOBI):
        sides = six_sides(jnp.pad(pressure, 1))
        flux = charge + coupling[0] * sides[0] + coupling[1] * sides[1] + coupling[2] * sides[2]
        flux = flux + coupling[3] * sides[3] + coupling[4] * sides[4] + coupling[5] * sides[5]
        pressure = flux / total
    slots = jnp.arange(N_GX * FLOW_MOST, dtype=jnp.int32)
    owners = slots // FLOW_MOST
    offsets = slots - owners * FLOW_MOST
    counts = bounds[1:] - bounds[:-1]
    valid = offsets < counts[owners]
    plane_of = jnp.clip(bounds[owners] + offsets, 0, NX_IN - 1).astype(jnp.int32)
    flow = jnp.where(valid[:, None, None], pressure[plane_of], 0.0)
    return field, flow
```

```python
import functools

import jax
import jax.numpy as jnp
from jax import lax
from jax.experimental import pallas as pl
from jax.experimental.pallas import tpu as pltpu
from jax.sharding import PartitionSpec as P

SWEEPS = 8
JACOBI = 8
THETA = 7.125
DELTA = 6.875
LOG_GAIN = 2.0
WIDE = 2
MESH = pl.DeviceIdType.MESH

OFFSETS = [
    (x, y, z)
    for x in (-1, 0, 1)
    for y in (-1, 0, 1)
    for z in (-1, 0, 1)
    if 1 <= abs(x) + abs(y) + abs(z) <= 2
]
OFFSETS.sort(key=lambda o: (o[2] != 0, abs(o[0]) + abs(o[1]) + abs(o[2]), -abs(o[0])))


def sweep_weights(count):
    ratio_base = THETA / DELTA
    ratio_now = 1.0 / ratio_base
    weights = []
    for index in range(count):
        ratio_next = 1.0 / (2.0 * ratio_base - ratio_now)
        weights.append((ratio_next * ratio_now, 2.0 * ratio_next / DELTA))
        ratio_now = ratio_next
    return weights


class Plan:
    def __init__(self, mesh, cells, flow_rows):
        self.size = (mesh.shape["gx"], mesh.shape["gy"], mesh.shape["gz"])
        self.cells = cells
        self.flow_rows = flow_rows
        self.inset = 3 * cells[0] * self.size[0] // 4
        cx, count = cells[0], self.size[0]
        mean = 3 * cx // 4
        jitter = (mean - 2) // 2
        centre = cx * count // 8
        self.shifts = {}
        for shift in range(1 - count, count):
            low, high = cx, 0
            for tile in range(max(0, -shift), min(count, count - shift)):
                begin = mean * tile + centre - 2 * jitter - cx * (tile + shift)
                end = begin + flow_rows + 2 * jitter
                if max(begin, 0) < min(end, cx):
                    low, high = min(low, max(begin, 0)), max(high, min(end, cx))
            if low < high:
                self.shifts[shift] = (low, high)
        self.shifts[0] = (0, cx)
        self.lowest, self.highest = min(self.shifts), max(self.shifts)
        self.moves = [s for s in sorted(self.shifts, key=abs) if s != 0]
        self.rounds = [(2, 2), (1, 2), (1, 2), (1, 1), (2, 2), (1, 2), (1, 2), (1, 2), (1, 2)]
        self.bases = [sum(n for n, _ in self.rounds[:i]) for i in range(len(self.rounds))]
        self.total = sum(n for n, _ in self.rounds)


def kernel(
    plan,
    cuts_ref, noise_ref, kappa_ref, init_ref, source_ref,
    field_ref, pressure_ref,
    dir_a, dir_b, resid, kap, prs_a, prs_b, coef, charge, perm, maskv,
    send, packed, land_x, land_y, land_xy, land_p,
    move_out, move_in, last, landed,
    send_sem, recv_sem, move_send, move_recv, last_send, last_recv,
):
    cx, cy, cz = plan.cells
    ext_x, ext_y = cx + 2 * WIDE, cy + 8
    me = [lax.axis_index("gx"), lax.axis_index("gy"), lax.axis_index("gz")]
    tiles_y = cy // 8

    def there(offset):
        flag = None
        for at, by, size in zip(me, offset, plan.size):
            if by == 0:
                continue
            one = (at + by < size) if by > 0 else (at + by >= 0)
            flag = one if flag is None else flag & one
        return flag

    def device(offset):
        return tuple(at + by for at, by in zip(me, offset))

    has = {o: there(o) for o in OFFSETS}
    greet = [o for o in OFFSETS] + [(s, 0, 0) for s in plan.moves if abs(s) > 1]
    for s in plan.moves:
        has[(s, 0, 0)] = there((s, 0, 0))
        has[(-s, 0, 0)] = there((-s, 0, 0))

    barrier = pltpu.get_barrier_semaphore()
    expected = jnp.int32(0)
    for o in greet:
        expected = expected + has[o].astype(jnp.int32)

        @pl.when(has[o])
        def _(o=o):
            pl.semaphore_signal(barrier, inc=1, device_id=device(o), device_id_type=MESH)

    pl.semaphore_wait(barrier, expected)

    lane = lax.broadcasted_iota(jnp.int32, (8, cz), 1)
    row8 = lax.broadcasted_iota(jnp.int32, (8, cz), 0)

    def offsets_of(width):
        return [(i, o) for i, o in enumerate(OFFSETS) if sum(map(abs, o)) <= width]

    def copy_of(rnd, index, o):
        n, w = plan.rounds[rnd]
        arrays = pl.ds(plan.bases[rnd], n)
        planes = {0: pl.ds(0, cx), 1: pl.ds(cx - w, w), -1: pl.ds(0, w)}[o[0]]
        rows = {0: pl.ds(0, cy), 1: pl.ds(cy - 8, 8), -1: pl.ds(0, 8)}[o[1]]
        fx, fy = (0 if o[0] > 0 else 1), (0 if o[1] > 0 else 1)
        if o[2] != 0:
            side = 0 if o[2] < 0 else 1
            src = packed.at[side, arrays]
            dst = land_p.at[1 - o[0], 1 - o[1], side, arrays]
        elif o[0] != 0 and o[1] != 0:
            src = send.at[arrays, planes, rows]
            dst = land_xy.at[fx, fy, arrays, pl.ds(0, w)]
        elif o[0] != 0:
            src = send.at[arrays, planes, rows]
            dst = land_x.at[fx, arrays, pl.ds(0, w)]
        else:
            src = send.at[arrays, planes, rows]
            dst = land_y.at[fy, arrays]
        return pltpu.make_async_remote_copy(
            src_ref=src, dst_ref=dst,
            send_sem=send_sem.at[rnd, index], recv_sem=recv_sem.at[rnd, index],
            device_id=device(o), device_id_type=MESH,
        )

    def start(rnd):
        n, w = plan.rounds[rnd]

        def begin(index, o):
            @pl.when(has[o])
            def _():
                copy_of(rnd, index, o).start()

        for index, o in offsets_of(w):
            if o[2] == 0:
                begin(index, o)
        for a in range(n):
            slot = plan.bases[rnd] + a
            low = jnp.zeros((8, cz), jnp.float32)
            high = jnp.zeros((8, cz), jnp.float32)
            for k in range(cx):
                for j in range(tiles_y):
                    by = (j * cx + k) * w
                    value = send[slot, k, 8 * j : 8 * j + 8]
                    low = jnp.where((lane >= by) & (lane < by + w), pltpu.roll(value, by, 1), low)
                    back = (cz - by) % cz
                    high = jnp.where(
                        (lane >= cz - w - by) & (lane < cz - by), pltpu.roll(value, back, 1), high
                    )
            packed[0, slot] = low
            packed[1, slot] = high
        for index, o in offsets_of(w):
            if o[2] != 0:
                begin(index, o)

    def finish(rnd):
        n, w = plan.rounds[rnd]
        for index, o in offsets_of(w):
            back = tuple(-v for v in o)

            @pl.when(has[back])
            def _(index=index, o=o):
                copy_of(rnd, index, o).wait_recv()

        for index, o in offsets_of(w):
            @pl.when(has[o])
            def _(index=index, o=o):
                copy_of(rnd, index, o).wait_send()

    def assemble(rnd, a, put, fill=0.0):
        n, w = plan.rounds[rnd]
        slot = plan.bases[rnd] + a
        blank = jnp.full((8, cz), fill, jnp.float32)
        arrived = {}
        for o in OFFSETS:
            if o[2] != 0 and sum(map(abs, o)) <= w:
                side = 0 if o[2] > 0 else 1
                arrived[o] = jnp.where(has[o], land_p[1 + o[0], 1 + o[1], side, slot], blank)

        def unpack(dx, dy, k, j):
            by = (j * cx + k) * w
            value = blank
            if (dx, dy, 1) in arrived:
                right = pltpu.roll(arrived[dx, dy, 1], (cz - by) % cz, 1)
                value = jnp.where(lane < w, right, value)
                left = pltpu.roll(arrived[dx, dy, -1], by, 1)
                value = jnp.where(lane >= cz - w, left, value)
            return value

        def between(after, before):
            return jnp.where(row8 < w, after, jnp.where(row8 >= 8 - w, before, blank))

        def columns(dx, k, plane):
            for j in range(tiles_y):
                put(1, plane, 8 * j, unpack(dx, 0, k, j))
            put(1, plane, cy, between(unpack(dx, 1, k, 0), unpack(dx, -1, k, tiles_y - 1)))

        for k in range(cx):
            after = jnp.where(has[0, 1, 0], land_y[1, slot, k], blank)
            before = jnp.where(has[0, -1, 0], land_y[0, slot, k], blank)
            put(0, WIDE + k, cy, between(after, before))
            columns(0, k, WIDE + k)
        for dx in (-1, 1):
            fx = 0 if dx < 0 else 1
            for q in range(w):
                plane = WIDE - w + q if dx < 0 else WIDE + cx + q
                k = cx - w + q if dx < 0 else q
                big = jnp.where(has[dx, 0, 0], land_x[fx, slot, q], jnp.full((cy, cz), fill, jnp.float32))
                for j in range(tiles_y):
                    put(0, plane, 8 * j, big[8 * j : 8 * j + 8])
                if w > 1:
                    after = jnp.where(has[dx, 1, 0], land_xy[fx, 1, slot, q], blank)
                    before = jnp.where(has[dx, -1, 0], land_xy[fx, 0, slot, q], blank)
                    put(0, plane, cy, between(after, before))
                    columns(dx, k, plane)
                else:
                    put(0, plane, cy, blank)
                    for j in range(tiles_y + 1):
                        put(1, plane, 8 * j, blank)

    send[0] = noise_ref[...]
    send[1] = kappa_ref[...]
    start(0)

    inset_begin = cuts_ref[0]
    cut_here = cuts_ref[me[0] + 1]
    count_here = cuts_ref[me[0] + 2] - cut_here

    def pick(ref, shift, r):
        row = cx * (me[0] + shift) + r - inset_begin - cut_here
        value = ref[jnp.clip(row, 0, plan.flow_rows - 1)]
        return jnp.where((row >= 0) & (row < count_here), value, 0.0)

    def move_of(index, shift):
        low, high = plan.shifts[shift]
        return pltpu.make_async_remote_copy(
            src_ref=move_out.at[index, :, pl.ds(low, high - low)],
            dst_ref=move_in.at[index, :, pl.ds(low, high - low)],
            send_sem=move_send.at[index], recv_sem=move_recv.at[index],
            device_id=device((shift, 0, 0)), device_id_type=MESH,
        )

    for index, shift in enumerate(plan.moves):
        low, high = plan.shifts[shift]
        for a, ref in enumerate((init_ref, source_ref)):
            @pl.loop(low, high)
            def _(r, a=a, ref=ref, index=index, shift=shift):
                move_out[index, a, r] = pick(ref, shift, r)

        @pl.when(has[shift, 0, 0])
        def _(index=index, shift=shift):
            move_of(index, shift).start()

    slot_q = plan.bases[4]
    for a, ref in enumerate((init_ref, source_ref)):
        @pl.loop(0, cx)
        def _(r, a=a, ref=ref):
            send[slot_q + a, r] = pick(ref, 0, r)

    row = lax.broadcasted_iota(jnp.int32, (ext_y, cz), 0)
    col = lax.broadcasted_iota(jnp.int32, (ext_y, cz), 1)
    in_rows = (row < cy) | ((row < cy + WIDE) & has[0, 1, 0]) | ((row >= ext_y - WIDE) & has[0, -1, 0])
    in_cols = ((col < WIDE) & has[0, 0, 1]) | ((col >= cz - WIDE) & has[0, 0, -1])
    maskv[0] = jnp.where(in_rows, 1.0, 0.0)
    maskv[1] = jnp.where(in_rows & in_cols, 1.0, 0.0)

    for k in range(cx):
        value = noise_ref[k]
        resid[0, WIDE + k, 0:cy] = value
        dir_a[0, WIDE + k, 0:cy] = value * (1.0 / THETA)
        field_ref[k] = value * (1.0 / THETA)
        kap[0, WIDE + k, 0:cy] = kappa_ref[k] + 6.0

    first_col, last_col = col == 0, col == cz - 1

    def sides(ref, e):
        core, outer = ref[0, e], ref[1, e]
        core_r, outer_r = pltpu.roll(core, cz - 1, 1), pltpu.roll(outer, cz - 1, 1)
        core_l, outer_l = pltpu.roll(core, 1, 1), pltpu.roll(outer, 1, 1)
        return (
            (core, pltpu.roll(core, 1, 0), pltpu.roll(core, ext_y - 1, 0),
             jnp.where(first_col, outer_l, core_l), jnp.where(last_col, outer_r, core_r)),
            (outer, pltpu.roll(outer, 1, 0), pltpu.roll(outer, ext_y - 1, 0),
             jnp.where(first_col, core_l, outer_l), jnp.where(last_col, core_r, outer_r)),
        )

    weights = sweep_weights(SWEEPS)

    def inside(e):
        at = me[0] * cx - WIDE + e
        return (at >= 0) & (at < plan.size[0] * cx)

    def cheb_wide(old, new, weight):
        @pl.loop(1, ext_x - 1)
        def _(e):
            okay = jnp.where(inside(e), 1.0, 0.0)
            for zt, (mid, up, down, left, right) in enumerate(sides(old, e)):
                beside = old[zt, e - 1] + old[zt, e + 1] + (up + down) + (left + right)
                change = (kap[zt, e] * mid - beside) * (maskv[zt] * okay)
                rest = resid[zt, e] - change
                resid[zt, e] = rest
                new[zt, e] = weight[0] * mid + weight[1] * rest

        @pl.loop(0, cx)
        def _(k):
            field_ref[k] = field_ref[k] + new[0, k + WIDE, 0:cy]

    def cheb_core(old, new, weight, slot):
        @pl.loop(0, cx)
        def _(k):
            e = k + WIDE
            mid, up, down, left, right = sides(old, e)[0]
            beside = old[0, e - 1] + old[0, e + 1] + (up + down) + (left + right)
            rest = (resid[0, e] - (kap[0, e] * mid - beside))[0:cy]
            resid[0, e, 0:cy] = rest
            value = weight[0] * mid[0:cy] + weight[1] * rest
            total = field_ref[k] + value
            field_ref[k] = total
            if slot is None:
                raised = jnp.exp(LOG_GAIN * total)
                send[plan.bases[5], k] = raised
                perm[0, e, 0:cy] = raised
            else:
                new[0, e, 0:cy] = value
                send[slot, k] = value

    finish(0)

    def put_noise(zt, e, r, value):
        resid[zt, e, r : r + 8] = value
        dir_a[zt, e, r : r + 8] = value * (1.0 / THETA)

    def put_kappa(zt, e, r, value):
        kap[zt, e, r : r + 8] = value + 6.0

    assemble(0, 0, put_noise)
    assemble(0, 1, put_kappa)
    cheb_wide(dir_a, dir_b, weights[0])
    cheb_core(dir_b, dir_a, weights[1], plan.bases[1])
    start(1)
    for rnd in (1, 2):
        before = weights[2 * rnd - 1]

        def put_dir(zt, e, r, value, before=before):
            dir_a[zt, e, r : r + 8] = value
            if 1 <= e < ext_x - 1:
                resid[zt, e, r : r + 8] = (value - before[0] * dir_b[zt, e, r : r + 8]) * (1.0 / before[1])

        if rnd == 2:
            for index, shift in enumerate(plan.moves):
                low, high = plan.shifts[shift]

                @pl.when(has[-shift, 0, 0])
                def _(index=index, shift=shift, low=low, high=high):
                    move_of(index, shift).wait_recv()
                    for a in range(2):
                        send[slot_q + a, low:high] = send[slot_q + a, low:high] + move_in[index, a, low:high]

                @pl.when(has[shift, 0, 0])
                def _(index=index, shift=shift):
                    move_of(index, shift).wait_send()

            start(4)
        finish(rnd)
        assemble(rnd, 0, put_dir)
        cheb_wide(dir_a, dir_b, weights[2 * rnd])
        cheb_core(dir_b, dir_a, weights[2 * rnd + 1], plan.bases[rnd + 1])
        start(rnd + 1)

    def put_last(zt, e, r, value):
        dir_a[zt, e, r : r + 8] = value

    finish(3)
    assemble(3, 0, put_last)
    cheb_core(dir_a, None, weights[6], None)
    start(5)

    finish(4)

    def put_init(zt, e, r, value):
        prs_a[zt, e, r : r + 8] = value

    def put_charge(zt, e, r, value):
        charge[zt, e, r : r + 8] = value

    assemble(4, 0, put_init)
    assemble(4, 1, put_charge)
    for k in range(cx):
        prs_a[0, WIDE + k, 0:cy] = send[slot_q, k]
        charge[0, WIDE + k, 0:cy] = send[slot_q + 1, k]

    finish(5)

    def put_perm(zt, e, r, value):
        perm[zt, e, r : r + 8] = value

    assemble(5, 0, put_perm, fill=1.0)

    top = (row == 0) & (me[1] == 0)
    bottom = (row == cy - 1) & (me[1] == plan.size[1] - 1)
    near = first_col & (me[2] == 0)
    far = last_col & (me[2] == plan.size[2] - 1)

    def harmonic(own, other):
        return 2.0 * own * other / (own + other)

    @pl.loop(1, ext_x - 1)
    def _(e):
        plane = me[0] * cx - WIDE + e - inset_begin
        okay = (plane >= 0) & (plane < plan.inset)
        for zt, (mid, up, down, left, right) in enumerate(sides(perm, e)):
            below = jnp.where(plane == 0, mid, perm[zt, e - 1])
            above = jnp.where(plane == plan.inset - 1, mid, perm[zt, e + 1])
            up = jnp.where(top, mid, up)
            down = jnp.where(bottom, mid, down)
            if zt == 0:
                left = jnp.where(near, mid, left)
                right = jnp.where(far, mid, right)
            parts = [harmonic(mid, v) for v in (below, above, up, down, left, right)]
            total = parts[0] + parts[1] + parts[2] + parts[3] + parts[4] + parts[5]
            valid = (maskv[zt] > 0.5) & okay
            for f in range(6):
                coef[f, zt, e] = jnp.where(valid, parts[f] / total, 0.0)
            charge[zt, e] = jnp.where(valid, charge[zt, e] / total, 0.0)

    def flux(old, zt, e, around):
        _, up, down, left, right = around
        value = charge[zt, e] + coef[0, zt, e] * old[zt, e - 1] + coef[1, zt, e] * old[zt, e + 1]
        value = value + coef[2, zt, e] * up + coef[3, zt, e] * down
        return value + coef[4, zt, e] * left + coef[5, zt, e] * right

    def jacobi_wide(old, new):
        @pl.loop(1, ext_x - 1)
        def _(e):
            for zt, around in enumerate(sides(old, e)):
                new[zt, e] = flux(old, zt, e, around)

    def jacobi_core(old, new, slot):
        @pl.loop(0, cx)
        def _(k):
            e = k + WIDE
            value = flux(old, 0, e, sides(old, e)[0])[0:cy]
            if slot is None:
                last[k] = value
            else:
                new[0, e, 0:cy] = value
                send[slot, k] = value

    for block in range(JACOBI // 2):
        if block > 0:
            finish(5 + block)
            assemble(5 + block, 0, put_init)
        jacobi_wide(prs_a, prs_b)
        final = block == JACOBI // 2 - 1
        jacobi_core(prs_b, prs_a, None if final else plan.bases[6 + block])
        if not final:
            start(6 + block)

    def last_of(index, shift):
        low, high = plan.shifts[shift]
        at = (shift - plan.lowest) * cx + low
        return pltpu.make_async_remote_copy(
            src_ref=last.at[pl.ds(low, high - low)],
            dst_ref=landed.at[pl.ds(at, high - low)],
            send_sem=last_send.at[index], recv_sem=last_recv.at[index],
            device_id=device((-shift, 0, 0)), device_id_type=MESH,
        )

    for index, shift in enumerate(plan.moves):
        @pl.when(has[-shift, 0, 0])
        def _(index=index, shift=shift):
            last_of(index, shift).start()

    landed[-plan.lowest * cx : (1 - plan.lowest) * cx] = last[...]
    for index, shift in enumerate(plan.moves):
        @pl.when(has[shift, 0, 0])
        def _(index=index, shift=shift):
            last_of(index, shift).wait_recv()

    window = (plan.highest - plan.lowest + 1) * cx

    @pl.loop(0, plan.flow_rows)
    def _(j):
        at = inset_begin + cut_here + j - cx * (me[0] + plan.lowest)
        value = landed[jnp.clip(at, 0, window - 1)]
        pressure_ref[j] = jnp.where(j < count_here, value, 0.0)

    for index, shift in enumerate(plan.moves):
        @pl.when(has[-shift, 0, 0])
        def _(index=index, shift=shift):
            last_of(index, shift).wait_send()


def local(mesh, noise, kappa_sq, cuts, pressure_init, source):
    cells, flow_rows = noise.shape, pressure_init.shape[0]
    plan = Plan(mesh, cells, flow_rows)
    cx, cy, cz = cells
    block = (2, cx + 2 * WIDE, cy + 8, cz)
    moves = max(1, len(plan.moves))
    f32 = jnp.float32
    vmem = lambda *shape: pltpu.VMEM(shape, f32)
    sems = lambda *shape: pltpu.SemaphoreType.DMA(shape)
    total = plan.total
    return pl.pallas_call(
        functools.partial(kernel, plan),
        out_shape=(
            jax.ShapeDtypeStruct(noise.shape, f32),
            jax.ShapeDtypeStruct(pressure_init.shape, f32),
        ),
        in_specs=[pl.BlockSpec(memory_space=pltpu.SMEM)] + [pl.BlockSpec(memory_space=pltpu.VMEM)] * 4,
        out_specs=(pl.BlockSpec(memory_space=pltpu.VMEM),) * 2,
        scratch_shapes=[
            vmem(*block), vmem(*block), vmem(*block), vmem(*block), vmem(*block), vmem(*block),
            vmem(6, *block), vmem(*block), vmem(*block), vmem(2, cy + 8, cz),
            vmem(total, cx, cy, cz), vmem(2, total, 8, cz),
            vmem(2, total, WIDE, cy, cz), vmem(2, total, cx, 8, cz),
            vmem(2, 2, total, WIDE, 8, cz), vmem(3, 3, 2, total, 8, cz),
            vmem(moves, 2, cx, cy, cz), vmem(moves, 2, cx, cy, cz),
            vmem(cx, cy, cz), vmem((plan.highest - plan.lowest + 1) * cx, cy, cz),
            sems(len(plan.rounds), len(OFFSETS)), sems(len(plan.rounds), len(OFFSETS)),
            sems(moves), sems(moves), sems(moves), sems(moves),
        ],
        compiler_params=pltpu.CompilerParams(
            collective_id=0, has_side_effects=True, vmem_limit_bytes=48 * 1024 * 1024
        ),
        cost_estimate=pl.CostEstimate(flops=30_000_000, bytes_accessed=1_000_000, transcendentals=32768),
        name="sweeps",
    )(cuts, noise, kappa_sq, pressure_init, source)


def solution(mesh):
    part = P("gx", "gy", "gz")
    return jax.shard_map(
        functools.partial(local, mesh),
        mesh=mesh,
        in_specs=(part, part, P(), part, part),
        out_specs=(part, part),
        check_vma=False,
    )
```

```python
import functools

import jax
import jax.numpy as jnp
from jax import lax
from jax.experimental import pallas as pl
from jax.experimental.pallas import tpu as pltpu
from jax.sharding import PartitionSpec as P

SWEEPS = 8
JACOBI = 8
THETA = 7.125
DELTA = 6.875
LOG_GAIN = 2.0
WIDE = 4
MESH = pl.DeviceIdType.MESH

OFFSETS = [
    (x, y, z)
    for x in (-1, 0, 1)
    for y in (-1, 0, 1)
    for z in (-1, 0, 1)
    if abs(x) + abs(y) + abs(z) >= 1
]
OFFSETS.sort(key=lambda o: (o[2] != 0, abs(o[0]) + abs(o[1]) + abs(o[2]), -abs(o[0])))


def sweep_weights(count):
    ratio_base = THETA / DELTA
    ratio_now = 1.0 / ratio_base
    weights = []
    for index in range(count):
        ratio_next = 1.0 / (2.0 * ratio_base - ratio_now)
        weights.append((ratio_next * ratio_now, 2.0 * ratio_next / DELTA))
        ratio_now = ratio_next
    return weights


class Plan:
    def __init__(self, mesh, cells, flow_rows):
        self.size = (mesh.shape["gx"], mesh.shape["gy"], mesh.shape["gz"])
        self.cells = cells
        self.flow_rows = flow_rows
        self.inset = 3 * cells[0] * self.size[0] // 4
        cx, count = cells[0], self.size[0]
        mean = 3 * cx // 4
        jitter = (mean - 2) // 2
        centre = cx * count // 8
        self.shifts = {}
        for shift in range(1 - count, count):
            low, high = cx, 0
            for tile in range(max(0, -shift), min(count, count - shift)):
                begin = mean * tile + centre - 2 * jitter - cx * (tile + shift)
                end = begin + flow_rows + 2 * jitter
                if max(begin, 0) < min(end, cx):
                    low, high = min(low, max(begin, 0)), max(high, min(end, cx))
            if low < high:
                self.shifts[shift] = (low, high)
        self.shifts[0] = (0, cx)
        self.lowest, self.highest = min(self.shifts), max(self.shifts)
        self.moves = [s for s in sorted(self.shifts, key=abs) if s != 0]
        self.rounds = [(2, 4), (2, 3), (2, 4), (1, 4), (1, 4)]
        self.bases = [sum(n for n, _ in self.rounds[:i]) for i in range(len(self.rounds))]
        self.total = sum(n for n, _ in self.rounds)


def kernel(
    plan,
    cuts_hbm, noise_hbm, kappa_hbm, init_hbm, source_hbm,
    field_ref, pressure_ref,
    dir_a, dir_b, resid, kap, prs_a, prs_b, coef, charge, perm, maskv,
    init_in, source_in, cuts_in, load_sem,
    send, packed, land_x, land_y, land_xy, land_p,
    move_out, move_in, last, landed,
    send_sem, recv_sem, move_send, move_recv, last_send, last_recv,
):
    cx, cy, cz = plan.cells
    ext_x, ext_y = cx + 2 * WIDE, cy + 8
    me = [lax.axis_index("gx"), lax.axis_index("gy"), lax.axis_index("gz")]
    tiles_y = cy // 8

    def there(offset):
        flag = None
        for at, by, size in zip(me, offset, plan.size):
            if by == 0:
                continue
            one = (at + by < size) if by > 0 else (at + by >= 0)
            flag = one if flag is None else flag & one
        return flag

    def device(offset):
        return tuple(at + by for at, by in zip(me, offset))

    has = {o: there(o) for o in OFFSETS}
    greet = [o for o in OFFSETS] + [(s, 0, 0) for s in plan.moves if abs(s) > 1]
    for s in plan.moves:
        has[(s, 0, 0)] = there((s, 0, 0))
        has[(-s, 0, 0)] = there((-s, 0, 0))

    init_ref, source_ref, cuts_ref = init_in, source_in, cuts_in
    loads = [
        pltpu.make_async_copy(noise_hbm, send.at[0], load_sem.at[0]),
        pltpu.make_async_copy(kappa_hbm, send.at[1], load_sem.at[1]),
        pltpu.make_async_copy(init_hbm, init_in, load_sem.at[2]),
        pltpu.make_async_copy(source_hbm, source_in, load_sem.at[3]),
        pltpu.make_async_copy(cuts_hbm, cuts_in, load_sem.at[4]),
    ]
    for load in loads:
        load.start()

    barrier = pltpu.get_barrier_semaphore()
    expected = jnp.int32(0)
    for o in greet:
        expected = expected + has[o].astype(jnp.int32)

        @pl.when(has[o])
        def _(o=o):
            pl.semaphore_signal(barrier, inc=1, device_id=device(o), device_id_type=MESH)

    pl.semaphore_wait(barrier, expected)

    lane = lax.broadcasted_iota(jnp.int32, (8, cz), 1)
    row8 = lax.broadcasted_iota(jnp.int32, (8, cz), 0)

    def offsets_of(width):
        return [(i, o) for i, o in enumerate(OFFSETS) if sum(map(abs, o)) <= width]

    def copy_of(rnd, index, o):
        n, w = plan.rounds[rnd]
        arrays = pl.ds(plan.bases[rnd], n)
        planes = {0: pl.ds(0, cx), 1: pl.ds(cx - w, w), -1: pl.ds(0, w)}[o[0]]
        rows = {0: pl.ds(0, cy), 1: pl.ds(cy - 8, 8), -1: pl.ds(0, 8)}[o[1]]
        fx, fy = (0 if o[0] > 0 else 1), (0 if o[1] > 0 else 1)
        if o[2] != 0:
            side = 0 if o[2] < 0 else 1
            src = packed.at[side, arrays]
            dst = land_p.at[1 - o[0], 1 - o[1], side, arrays]
        elif o[0] != 0 and o[1] != 0:
            src = send.at[arrays, planes, rows]
            dst = land_xy.at[fx, fy, arrays, pl.ds(0, w)]
        elif o[0] != 0:
            src = send.at[arrays, planes, rows]
            dst = land_x.at[fx, arrays, pl.ds(0, w)]
        else:
            src = send.at[arrays, planes, rows]
            dst = land_y.at[fy, arrays]
        return pltpu.make_async_remote_copy(
            src_ref=src, dst_ref=dst,
            send_sem=send_sem.at[rnd, index], recv_sem=recv_sem.at[rnd, index],
            device_id=device(o), device_id_type=MESH,
        )

    def start(rnd):
        n, w = plan.rounds[rnd]

        def begin(index, o):
            @pl.when(has[o])
            def _():
                copy_of(rnd, index, o).start()

        for index, o in offsets_of(w):
            if o[2] == 0:
                begin(index, o)
        for a in range(n):
            slot = plan.bases[rnd] + a
            low = jnp.zeros((8, cz), jnp.float32)
            high = jnp.zeros((8, cz), jnp.float32)
            for k in range(cx):
                for j in range(tiles_y):
                    by = (j * cx + k) * w
                    value = send[slot, k, 8 * j : 8 * j + 8]
                    low = jnp.where((lane >= by) & (lane < by + w), pltpu.roll(value, by, 1), low)
                    back = (cz - by) % cz
                    high = jnp.where(
                        (lane >= cz - w - by) & (lane < cz - by), pltpu.roll(value, back, 1), high
                    )
            packed[0, slot] = low
            packed[1, slot] = high
        for index, o in offsets_of(w):
            if o[2] != 0:
                begin(index, o)

    def finish(rnd):
        n, w = plan.rounds[rnd]
        for index, o in offsets_of(w):
            back = tuple(-v for v in o)

            @pl.when(has[back])
            def _(index=index, o=o):
                copy_of(rnd, index, o).wait_recv()

        for index, o in offsets_of(w):
            @pl.when(has[o])
            def _(index=index, o=o):
                copy_of(rnd, index, o).wait_send()

    def assemble(rnd, a, put, fill=0.0):
        n, w = plan.rounds[rnd]
        slot = plan.bases[rnd] + a
        blank = jnp.full((8, cz), fill, jnp.float32)
        arrived = {}
        for o in OFFSETS:
            if o[2] != 0 and sum(map(abs, o)) <= w:
                side = 0 if o[2] > 0 else 1
                arrived[o] = jnp.where(has[o], land_p[1 + o[0], 1 + o[1], side, slot], blank)

        def unpack(dx, dy, k, j):
            by = (j * cx + k) * w
            value = blank
            if (dx, dy, 1) in arrived:
                right = pltpu.roll(arrived[dx, dy, 1], (cz - by) % cz, 1)
                value = jnp.where(lane < w, right, value)
                left = pltpu.roll(arrived[dx, dy, -1], by, 1)
                value = jnp.where(lane >= cz - w, left, value)
            return value

        def between(after, before):
            return jnp.where(row8 < w, after, jnp.where(row8 >= 8 - w, before, blank))

        def columns(dx, k, plane):
            for j in range(tiles_y):
                put(1, plane, 8 * j, unpack(dx, 0, k, j))
            put(1, plane, cy, between(unpack(dx, 1, k, 0), unpack(dx, -1, k, tiles_y - 1)))

        for k in range(cx):
            after = jnp.where(has[0, 1, 0], land_y[1, slot, k], blank)
            before = jnp.where(has[0, -1, 0], land_y[0, slot, k], blank)
            put(0, WIDE + k, cy, between(after, before))
            columns(0, k, WIDE + k)
        for dx in (-1, 1):
            fx = 0 if dx < 0 else 1
            for q in range(w):
                plane = WIDE - w + q if dx < 0 else WIDE + cx + q
                k = cx - w + q if dx < 0 else q
                big = jnp.where(has[dx, 0, 0], land_x[fx, slot, q], jnp.full((cy, cz), fill, jnp.float32))
                for j in range(tiles_y):
                    put(0, plane, 8 * j, big[8 * j : 8 * j + 8])
                if w > 1:
                    after = jnp.where(has[dx, 1, 0], land_xy[fx, 1, slot, q], blank)
                    before = jnp.where(has[dx, -1, 0], land_xy[fx, 0, slot, q], blank)
                    put(0, plane, cy, between(after, before))
                    columns(dx, k, plane)
                else:
                    put(0, plane, cy, blank)
                    for j in range(tiles_y + 1):
                        put(1, plane, 8 * j, blank)

    loads[0].wait()
    loads[1].wait()
    start(0)
    for load in loads[2:]:
        load.wait()

    inset_begin = cuts_ref[0]
    cut_here = cuts_ref[me[0] + 1]
    count_here = cuts_ref[me[0] + 2] - cut_here

    def pick(ref, shift, r):
        row = cx * (me[0] + shift) + r - inset_begin - cut_here
        value = ref[jnp.clip(row, 0, plan.flow_rows - 1)]
        return jnp.where((row >= 0) & (row < count_here), value, 0.0)

    def move_of(index, shift):
        low, high = plan.shifts[shift]
        return pltpu.make_async_remote_copy(
            src_ref=move_out.at[index, :, pl.ds(low, high - low)],
            dst_ref=move_in.at[index, :, pl.ds(low, high - low)],
            send_sem=move_send.at[index], recv_sem=move_recv.at[index],
            device_id=device((shift, 0, 0)), device_id_type=MESH,
        )

    for index, shift in enumerate(plan.moves):
        low, high = plan.shifts[shift]
        for a, ref in enumerate((init_ref, source_ref)):
            @pl.loop(low, high)
            def _(r, a=a, ref=ref, index=index, shift=shift):
                move_out[index, a, r] = pick(ref, shift, r)

        @pl.when(has[shift, 0, 0])
        def _(index=index, shift=shift):
            move_of(index, shift).start()

    slot_q = plan.bases[2]
    for a, ref in enumerate((init_ref, source_ref)):
        @pl.loop(0, cx)
        def _(r, a=a, ref=ref):
            send[slot_q + a, r] = pick(ref, 0, r)

    row = lax.broadcasted_iota(jnp.int32, (ext_y, cz), 0)
    col = lax.broadcasted_iota(jnp.int32, (ext_y, cz), 1)
    in_rows = (row < cy) | ((row < cy + WIDE) & has[0, 1, 0]) | ((row >= ext_y - WIDE) & has[0, -1, 0])
    in_cols = ((col < WIDE) & has[0, 0, 1]) | ((col >= cz - WIDE) & has[0, 0, -1])
    maskv[0] = jnp.where(in_rows, 1.0, 0.0)
    maskv[1] = jnp.where(in_rows & in_cols, 1.0, 0.0)

    for k in range(cx):
        value = send[0, k]
        resid[0, WIDE + k, 0:cy] = value
        dir_a[0, WIDE + k, 0:cy] = value * (1.0 / THETA)
        field_ref[k] = value * (1.0 / THETA)
        kap[0, WIDE + k, 0:cy] = send[1, k] + 6.0

    first_col, last_col = col == 0, col == cz - 1

    def sides(ref, e):
        core, outer = ref[0, e], ref[1, e]
        core_r, outer_r = pltpu.roll(core, cz - 1, 1), pltpu.roll(outer, cz - 1, 1)
        core_l, outer_l = pltpu.roll(core, 1, 1), pltpu.roll(outer, 1, 1)
        return (
            (core, pltpu.roll(core, 1, 0), pltpu.roll(core, ext_y - 1, 0),
             jnp.where(first_col, outer_l, core_l), jnp.where(last_col, outer_r, core_r)),
            (outer, pltpu.roll(outer, 1, 0), pltpu.roll(outer, ext_y - 1, 0),
             jnp.where(first_col, core_l, outer_l), jnp.where(last_col, core_r, outer_r)),
        )

    weights = sweep_weights(SWEEPS)

    def inside(e):
        at = me[0] * cx - WIDE + e
        return (at >= 0) & (at < plan.size[0] * cx)

    def planes_of(low, high):
        for first, end, own in ((low, WIDE, False), (WIDE, WIDE + cx, True), (WIDE + cx, high, False)):
            if first < end:
                yield first, end, own

    def cheb_wide(old, new, weight, low, high):
        for first, end, own in planes_of(low, high):
            @pl.loop(first, end, unroll=True)
            def _(e, own=own):
                okay = jnp.where(inside(e), 1.0, 0.0)
                for zt, (mid, up, down, left, right) in enumerate(sides(old, e)):
                    beside = old[zt, e - 1] + old[zt, e + 1] + (up + down) + (left + right)
                    part = maskv[zt] if own else maskv[zt] * okay
                    rest = resid[zt, e] - (kap[zt, e] * mid - beside) * part
                    resid[zt, e] = rest
                    value = weight[0] * mid + weight[1] * rest
                    new[zt, e] = value
                    if own and zt == 0:
                        field_ref[e - WIDE] = field_ref[e - WIDE] + value[0:cy]

    def cheb_core(old, new, weight, slot):
        @pl.loop(0, cx, unroll=True)
        def _(k):
            e = k + WIDE
            mid, up, down, left, right = sides(old, e)[0]
            beside = old[0, e - 1] + old[0, e + 1] + (up + down) + (left + right)
            rest = (resid[0, e] - (kap[0, e] * mid - beside))[0:cy]
            value = weight[0] * mid[0:cy] + weight[1] * rest
            total = field_ref[k] + value
            field_ref[k] = total
            if slot is None:
                raised = jnp.exp(LOG_GAIN * total)
                send[plan.bases[3], k] = raised
                perm[0, e, 0:cy] = raised
            else:
                resid[0, e, 0:cy] = rest
                new[0, e, 0:cy] = value
                send[slot, k] = value
                send[slot + 1, k] = rest

    finish(0)

    def put_noise(zt, e, r, value):
        resid[zt, e, r : r + 8] = value
        dir_a[zt, e, r : r + 8] = value * (1.0 / THETA)

    def put_kappa(zt, e, r, value):
        kap[zt, e, r : r + 8] = value + 6.0

    assemble(0, 0, put_noise)
    assemble(0, 1, put_kappa)
    for sweep in range(3):
        old, new = (dir_a, dir_b) if sweep % 2 == 0 else (dir_b, dir_a)
        cheb_wide(old, new, weights[sweep], sweep + 1, ext_x - sweep - 1)
    cheb_core(dir_b, dir_a, weights[3], plan.bases[1])
    start(1)

    for index, shift in enumerate(plan.moves):
        low, high = plan.shifts[shift]

        @pl.when(has[-shift, 0, 0])
        def _(index=index, shift=shift, low=low, high=high):
            move_of(index, shift).wait_recv()
            for a in range(2):
                send[slot_q + a, low:high] = send[slot_q + a, low:high] + move_in[index, a, low:high]

        @pl.when(has[shift, 0, 0])
        def _(index=index, shift=shift):
            move_of(index, shift).wait_send()

    start(2)

    def put_dir(zt, e, r, value):
        dir_a[zt, e, r : r + 8] = value

    def put_resid(zt, e, r, value):
        resid[zt, e, r : r + 8] = value

    finish(1)
    assemble(1, 0, put_dir)
    assemble(1, 1, put_resid)
    cheb_wide(dir_a, dir_b, weights[4], 2, ext_x - 2)
    cheb_wide(dir_b, dir_a, weights[5], 3, ext_x - 3)
    cheb_core(dir_a, None, weights[6], None)
    start(3)

    finish(2)

    def put_init(zt, e, r, value):
        prs_a[zt, e, r : r + 8] = value

    def put_charge(zt, e, r, value):
        charge[zt, e, r : r + 8] = value

    assemble(2, 0, put_init)
    assemble(2, 1, put_charge)
    for k in range(cx):
        prs_a[0, WIDE + k, 0:cy] = send[slot_q, k]
        charge[0, WIDE + k, 0:cy] = send[slot_q + 1, k]

    finish(3)

    def put_perm(zt, e, r, value):
        perm[zt, e, r : r + 8] = value

    assemble(3, 0, put_perm, fill=1.0)

    top = (row == 0) & (me[1] == 0)
    bottom = (row == cy - 1) & (me[1] == plan.size[1] - 1)
    near = first_col & (me[2] == 0)
    far = last_col & (me[2] == plan.size[2] - 1)

    def harmonic(own, other):
        return 2.0 * own * other / (own + other)

    @pl.loop(0, ext_x - 1, unroll=True)
    def _(e):
        plane = me[0] * cx - WIDE + e - inset_begin
        pair = (plane >= 0) & (plane < plan.inset - 1)
        for zt in range(2):
            coef[0, zt, e] = jnp.where(pair, harmonic(perm[zt, e], perm[zt, e + 1]), 0.0)

    @pl.loop(1, ext_x - 1, unroll=True)
    def _(e):
        plane = me[0] * cx - WIDE + e - inset_begin
        okay = (plane >= 0) & (plane < plan.inset)
        (core, _, core_down, _, core_right), (outer, _, outer_down, _, outer_right) = sides(perm, e)
        core_z = jnp.where(okay, harmonic(core, core_right), 0.0)
        outer_z = jnp.where(okay, harmonic(outer, outer_right), 0.0)
        core_back, outer_back = pltpu.roll(core_z, 1, 1), pltpu.roll(outer_z, 1, 1)
        core_left = jnp.where(first_col, outer_back, core_back)
        outer_left = jnp.where(first_col, core_back, outer_back)
        core_left, core_fore = jnp.where(near, core, core_left), jnp.where(far, core, core_z)
        for zt, mid, down, z_left, z_right, z_pair in (
            (0, core, core_down, core_left, core_fore, core_z),
            (1, outer, outer_down, outer_left, outer_z, outer_z),
        ):
            below = jnp.where(plane == 0, mid, coef[0, zt, e - 1])
            above = jnp.where(plane == plan.inset - 1, mid, coef[0, zt, e])
            y_pair = jnp.where(okay, harmonic(mid, down), 0.0)
            y_up = jnp.where(top, mid, pltpu.roll(y_pair, 1, 0))
            y_down = jnp.where(bottom, mid, y_pair)
            total = below + above + y_up + y_down + z_left + z_right
            valid = (maskv[zt] > 0.5) & okay
            coef[1, zt, e] = y_pair
            coef[2, zt, e] = z_pair
            coef[3, zt, e] = jnp.where(valid, 1.0 / total, 0.0)

    def flux(old, e, outer_too):
        core, outer = old[0, e], old[1, e]
        core_z, outer_z = coef[2, 0, e], coef[2, 1, e]
        core_r, outer_r = pltpu.roll(core, cz - 1, 1), pltpu.roll(outer, cz - 1, 1)
        core_l, outer_l = pltpu.roll(core * core_z, 1, 1), pltpu.roll(outer * outer_z, 1, 1)
        along = [jnp.where(last_col, outer_r, core_r) * core_z + jnp.where(first_col, outer_l, core_l)]
        if outer_too:
            along.append(jnp.where(last_col, core_r, outer_r) * outer_z + jnp.where(first_col, core_l, outer_l))
        values = []
        for zt, value in enumerate(along):
            mid, y_pair = (core, outer)[zt], coef[1, zt, e]
            value = value + charge[zt, e]
            value = value + (coef[0, zt, e - 1] * old[zt, e - 1] + coef[0, zt, e] * old[zt, e + 1])
            value = value + (y_pair * pltpu.roll(mid, ext_y - 1, 0) + pltpu.roll(y_pair * mid, 1, 0))
            values.append(value * coef[3, zt, e])
        return values

    def jacobi_wide(old, new, low, high):
        @pl.loop(low, high, unroll=True)
        def _(e):
            for zt, value in enumerate(flux(old, e, True)):
                new[zt, e] = value

    def jacobi_core(old, new, slot):
        @pl.loop(0, cx, unroll=True)
        def _(k):
            e = k + WIDE
            value = flux(old, e, False)[0][0:cy]
            if slot is None:
                last[k] = value
            else:
                new[0, e, 0:cy] = value
                send[slot, k] = value

    for block in range(JACOBI // 4):
        final = block == JACOBI // 4 - 1
        if block > 0:
            finish(3 + block)
            assemble(3 + block, 0, put_init)
        for sweep in range(3):
            old, new = (prs_a, prs_b) if sweep % 2 == 0 else (prs_b, prs_a)
            jacobi_wide(old, new, sweep + 1, ext_x - sweep - 1)
        jacobi_core(prs_b, prs_a, None if final else plan.bases[4 + block])
        if not final:
            start(4 + block)

    def last_of(index, shift):
        low, high = plan.shifts[shift]
        at = (shift - plan.lowest) * cx + low
        return pltpu.make_async_remote_copy(
            src_ref=last.at[pl.ds(low, high - low)],
            dst_ref=landed.at[pl.ds(at, high - low)],
            send_sem=last_send.at[index], recv_sem=last_recv.at[index],
            device_id=device((-shift, 0, 0)), device_id_type=MESH,
        )

    for index, shift in enumerate(plan.moves):
        @pl.when(has[-shift, 0, 0])
        def _(index=index, shift=shift):
            last_of(index, shift).start()

    landed[-plan.lowest * cx : (1 - plan.lowest) * cx] = last[...]
    for index, shift in enumerate(plan.moves):
        @pl.when(has[shift, 0, 0])
        def _(index=index, shift=shift):
            last_of(index, shift).wait_recv()

    window = (plan.highest - plan.lowest + 1) * cx

    @pl.loop(0, plan.flow_rows)
    def _(j):
        at = inset_begin + cut_here + j - cx * (me[0] + plan.lowest)
        value = landed[jnp.clip(at, 0, window - 1)]
        pressure_ref[j] = jnp.where(j < count_here, value, 0.0)

    for index, shift in enumerate(plan.moves):
        @pl.when(has[-shift, 0, 0])
        def _(index=index, shift=shift):
            last_of(index, shift).wait_send()


def local(mesh, noise, kappa_sq, cuts, pressure_init, source):
    cells, flow_rows = noise.shape, pressure_init.shape[0]
    plan = Plan(mesh, cells, flow_rows)
    cx, cy, cz = cells
    block = (2, cx + 2 * WIDE, cy + 8, cz)
    moves = max(1, len(plan.moves))
    f32 = jnp.float32
    vmem = lambda *shape: pltpu.VMEM(shape, f32)
    sems = lambda *shape: pltpu.SemaphoreType.DMA(shape)
    total = plan.total
    return pl.pallas_call(
        functools.partial(kernel, plan),
        out_shape=(
            jax.ShapeDtypeStruct(noise.shape, f32),
            jax.ShapeDtypeStruct(pressure_init.shape, f32),
        ),
        in_specs=[pl.BlockSpec(memory_space=pl.ANY)] * 5,
        out_specs=(pl.BlockSpec(memory_space=pltpu.VMEM),) * 2,
        scratch_shapes=[
            vmem(*block), vmem(*block), vmem(*block), vmem(*block), vmem(*block), vmem(*block),
            vmem(4, *block), vmem(*block), vmem(*block), vmem(2, cy + 8, cz),
            vmem(*pressure_init.shape), vmem(*source.shape),
            pltpu.SMEM(cuts.shape, jnp.int32), sems(5),
            vmem(total, cx, cy, cz), vmem(2, total, 8, cz),
            vmem(2, total, WIDE, cy, cz), vmem(2, total, cx, 8, cz),
            vmem(2, 2, total, WIDE, 8, cz), vmem(3, 3, 2, total, 8, cz),
            vmem(moves, 2, cx, cy, cz), vmem(moves, 2, cx, cy, cz),
            vmem(cx, cy, cz), vmem((plan.highest - plan.lowest + 1) * cx, cy, cz),
            sems(len(plan.rounds), len(OFFSETS)), sems(len(plan.rounds), len(OFFSETS)),
            sems(moves), sems(moves), sems(moves), sems(moves),
        ],
        compiler_params=pltpu.CompilerParams(
            collective_id=0, has_side_effects=True, vmem_limit_bytes=48 * 1024 * 1024
        ),
        cost_estimate=pl.CostEstimate(flops=30_000_000, bytes_accessed=1_000_000, transcendentals=32768),
        name="sweeps",
    )(cuts, noise, kappa_sq, pressure_init, source)


def solution(mesh):
    part = P("gx", "gy", "gz")
    return jax.shard_map(
        functools.partial(local, mesh),
        mesh=mesh,
        in_specs=(part, part, P(), part, part),
        out_specs=(part, part),
        check_vma=False,
    )
```

```python
import functools

import jax
import jax.numpy as jnp
from jax import lax
from jax.experimental import pallas as pl
from jax.experimental.pallas import tpu as pltpu
from jax.sharding import PartitionSpec as P

SWEEPS = 8
JACOBI = 8
THETA = 7.125
DELTA = 6.875
LOG_GAIN = 2.0
WIDE = 4
MESH = pl.DeviceIdType.MESH

OFFSETS = [
    (x, y, z)
    for x in (-1, 0, 1)
    for y in (-1, 0, 1)
    for z in (-1, 0, 1)
    if abs(x) + abs(y) + abs(z) >= 1
]
OFFSETS.sort(key=lambda o: (o[2] != 0, abs(o[0]) + abs(o[1]) + abs(o[2]), -abs(o[0])))


def sweep_weights(count):
    ratio_base = THETA / DELTA
    ratio_now = 1.0 / ratio_base
    weights = []
    for index in range(count):
        ratio_next = 1.0 / (2.0 * ratio_base - ratio_now)
        weights.append((ratio_next * ratio_now, 2.0 * ratio_next / DELTA))
        ratio_now = ratio_next
    return weights


class Plan:
    def __init__(self, mesh, cells, flow_rows):
        self.size = (mesh.shape["gx"], mesh.shape["gy"], mesh.shape["gz"])
        self.cells = cells
        self.flow_rows = flow_rows
        self.inset = 3 * cells[0] * self.size[0] // 4
        cx, count = cells[0], self.size[0]
        mean = 3 * cx // 4
        jitter = (mean - 2) // 2
        centre = cx * count // 8
        self.shifts = {}
        for shift in range(1 - count, count):
            low, high = cx, 0
            for tile in range(max(0, -shift), min(count, count - shift)):
                begin = mean * tile + centre - 2 * jitter - cx * (tile + shift)
                end = begin + flow_rows + 2 * jitter
                if max(begin, 0) < min(end, cx):
                    low, high = min(low, max(begin, 0)), max(high, min(end, cx))
            if low < high:
                self.shifts[shift] = (low, high)
        self.shifts[0] = (0, cx)
        self.lowest, self.highest = min(self.shifts), max(self.shifts)
        self.moves = [s for s in sorted(self.shifts, key=abs) if s != 0]
        self.rounds = [(2, 4), (2, 3), (2, 4), (1, 4), (1, 4)]
        self.bases = [sum(n for n, _ in self.rounds[:i]) for i in range(len(self.rounds))]
        self.total = sum(n for n, _ in self.rounds)


def kernel(
    plan,
    cuts_hbm, noise_hbm, kappa_hbm, init_hbm, source_hbm,
    field_ref, pressure_ref,
    dirs, resid, kap, press, coef, charge, perm, maskv,
    init_in, source_in, cuts_in, load_sem,
    send, packed, land_x, land_y, land_xy, land_p,
    move_out, move_in, last, landed,
    send_sem, recv_sem, move_send, move_recv, last_send, last_recv,
):
    cx, cy, cz = plan.cells
    ext_x, ext_y = cx + 2 * WIDE, cy + 8
    me = [lax.axis_index("gx"), lax.axis_index("gy"), lax.axis_index("gz")]
    tiles_y = cy // 8

    def there(offset):
        flag = None
        for at, by, size in zip(me, offset, plan.size):
            if by == 0:
                continue
            one = (at + by < size) if by > 0 else (at + by >= 0)
            flag = one if flag is None else flag & one
        return flag

    def device(offset):
        return tuple(at + by for at, by in zip(me, offset))

    has = {o: there(o) for o in OFFSETS}
    greet = [o for o in OFFSETS] + [(s, 0, 0) for s in plan.moves if abs(s) > 1]
    for s in plan.moves:
        has[(s, 0, 0)] = there((s, 0, 0))
        has[(-s, 0, 0)] = there((-s, 0, 0))

    init_ref, source_ref, cuts_ref = init_in, source_in, cuts_in
    loads = [
        pltpu.make_async_copy(noise_hbm, send.at[0], load_sem.at[0]),
        pltpu.make_async_copy(kappa_hbm, send.at[1], load_sem.at[1]),
        pltpu.make_async_copy(init_hbm, init_in, load_sem.at[2]),
        pltpu.make_async_copy(source_hbm, source_in, load_sem.at[3]),
        pltpu.make_async_copy(cuts_hbm, cuts_in, load_sem.at[4]),
    ]
    for load in loads:
        load.start()

    barrier = pltpu.get_barrier_semaphore()
    expected = jnp.int32(0)
    for o in greet:
        expected = expected + has[o].astype(jnp.int32)

        @pl.when(has[o])
        def _(o=o):
            pl.semaphore_signal(barrier, inc=1, device_id=device(o), device_id_type=MESH)

    pl.semaphore_wait(barrier, expected)

    dir_l, prs_l = [dirs.at[i] for i in range(4)], [press.at[i] for i in range(4)]
    dir_a, prs_a = dir_l[0], prs_l[0]
    lane = lax.broadcasted_iota(jnp.int32, (8, cz), 1)
    row8 = lax.broadcasted_iota(jnp.int32, (8, cz), 0)

    def offsets_of(width):
        return [(i, o) for i, o in enumerate(OFFSETS) if sum(map(abs, o)) <= width]

    def copies_of(rnd):
        n, w = plan.rounds[rnd]
        listed = [(i, o, 0) for i, o in offsets_of(w)]
        if n > 1:
            extra = [o for o in OFFSETS if o[1] == 0 and o[2] == 0]
            listed = [(len(OFFSETS) + i, o, 1) for i, o in enumerate(extra)] + listed
        return sorted(listed, key=lambda c: (c[1][2] != 0, c[1][0] == 0 or c[1][1] != 0, c[2]))

    def copy_of(rnd, index, o, a):
        n, w = plan.rounds[rnd]
        arrays = pl.ds(plan.bases[rnd], n)
        if o[0] != 0 and o[1] == 0 and o[2] == 0:
            w, arrays = w - a, pl.ds(plan.bases[rnd] + a, 1)
        planes = {0: pl.ds(0, cx), 1: pl.ds(cx - w, w), -1: pl.ds(0, w)}[o[0]]
        rows = {0: pl.ds(0, cy), 1: pl.ds(cy - 8, 8), -1: pl.ds(0, 8)}[o[1]]
        fx, fy = (0 if o[0] > 0 else 1), (0 if o[1] > 0 else 1)
        if o[2] != 0:
            side = 0 if o[2] < 0 else 1
            src = packed.at[side, arrays]
            dst = land_p.at[1 - o[0], 1 - o[1], side, arrays]
        elif o[0] != 0 and o[1] != 0:
            src = send.at[arrays, planes, rows]
            dst = land_xy.at[fx, fy, arrays, pl.ds(0, w)]
        elif o[0] != 0:
            src = send.at[arrays, planes, rows]
            dst = land_x.at[fx, arrays, pl.ds(0, w)]
        else:
            src = send.at[arrays, planes, rows]
            dst = land_y.at[fy, arrays]
        return pltpu.make_async_remote_copy(
            src_ref=src, dst_ref=dst,
            send_sem=send_sem.at[rnd, index], recv_sem=recv_sem.at[rnd, index],
            device_id=device(o), device_id_type=MESH,
        )

    def start(rnd):
        n, w = plan.rounds[rnd]

        def begin(index, o, a):
            @pl.when(has[o])
            def _():
                copy_of(rnd, index, o, a).start()

        for index, o, a in copies_of(rnd):
            if o[2] == 0:
                begin(index, o, a)
        for a in range(n):
            slot = plan.bases[rnd] + a
            low = jnp.zeros((8, cz), jnp.float32)
            high = jnp.zeros((8, cz), jnp.float32)
            for k in range(cx):
                for j in range(tiles_y):
                    by = (j * cx + k) * w
                    value = send[slot, k, 8 * j : 8 * j + 8]
                    low = jnp.where((lane >= by) & (lane < by + w), pltpu.roll(value, by, 1), low)
                    back = (cz - by) % cz
                    high = jnp.where(
                        (lane >= cz - w - by) & (lane < cz - by), pltpu.roll(value, back, 1), high
                    )
            packed[0, slot] = low
            packed[1, slot] = high
        for index, o, a in copies_of(rnd):
            if o[2] != 0:
                begin(index, o, a)

    def finish(rnd, beside):
        for index, o, a in copies_of(rnd):
            if (o[0] == 0) == beside:
                @pl.when(has[tuple(-v for v in o)])
                def _(index=index, o=o, a=a):
                    copy_of(rnd, index, o, a).wait_recv()

    def let_go(rnd):
        for index, o, a in copies_of(rnd):
            @pl.when(has[o])
            def _(index=index, o=o, a=a):
                copy_of(rnd, index, o, a).wait_send()

    def assemble(rnd, a, put, beside, fill=0.0):
        n, w = plan.rounds[rnd]
        slot = plan.bases[rnd] + a
        blank = jnp.full((8, cz), fill, jnp.float32)
        arrived = {}
        for o in OFFSETS:
            if o[2] != 0 and sum(map(abs, o)) <= w and (o[0] == 0) == beside:
                side = 0 if o[2] > 0 else 1
                arrived[o] = jnp.where(has[o], land_p[1 + o[0], 1 + o[1], side, slot], blank)

        def unpack(dx, dy, k, j):
            by = (j * cx + k) * w
            value = blank
            if (dx, dy, 1) in arrived:
                right = pltpu.roll(arrived[dx, dy, 1], (cz - by) % cz, 1)
                value = jnp.where(lane < w, right, value)
                left = pltpu.roll(arrived[dx, dy, -1], by, 1)
                value = jnp.where(lane >= cz - w, left, value)
            return value

        def between(after, before):
            return jnp.where(row8 < w, after, jnp.where(row8 >= 8 - w, before, blank))

        def columns(dx, k, plane):
            for j in range(tiles_y):
                put(1, plane, 8 * j, unpack(dx, 0, k, j))
            put(1, plane, cy, between(unpack(dx, 1, k, 0), unpack(dx, -1, k, tiles_y - 1)))

        for k in range(cx) if beside else ():
            after = jnp.where(has[0, 1, 0], land_y[1, slot, k], blank)
            before = jnp.where(has[0, -1, 0], land_y[0, slot, k], blank)
            put(0, WIDE + k, cy, between(after, before))
            columns(0, k, WIDE + k)
        wide = w - a
        for dx in () if beside else (-1, 1):
            fx = 0 if dx < 0 else 1
            for q in range(wide):
                plane = WIDE - wide + q if dx < 0 else WIDE + cx + q
                k = cx - wide + q if dx < 0 else q
                i = q + a if dx < 0 else q
                big = jnp.where(has[dx, 0, 0], land_x[fx, slot, q], jnp.full((cy, cz), fill, jnp.float32))
                for j in range(tiles_y):
                    put(0, plane, 8 * j, big[8 * j : 8 * j + 8])
                after = jnp.where(has[dx, 1, 0], land_xy[fx, 1, slot, i], blank)
                before = jnp.where(has[dx, -1, 0], land_xy[fx, 0, slot, i], blank)
                put(0, plane, cy, between(after, before))
                columns(dx, k, plane)

    loads[0].wait()
    loads[1].wait()
    start(0)
    for load in loads[2:]:
        load.wait()

    inset_begin = cuts_ref[0]
    cut_here = cuts_ref[me[0] + 1]
    count_here = cuts_ref[me[0] + 2] - cut_here

    def pick(ref, shift, r):
        row = cx * (me[0] + shift) + r - inset_begin - cut_here
        value = ref[jnp.clip(row, 0, plan.flow_rows - 1)]
        return jnp.where((row >= 0) & (row < count_here), value, 0.0)

    def move_of(index, shift):
        low, high = plan.shifts[shift]
        return pltpu.make_async_remote_copy(
            src_ref=move_out.at[index, :, pl.ds(low, high - low)],
            dst_ref=move_in.at[index, :, pl.ds(low, high - low)],
            send_sem=move_send.at[index], recv_sem=move_recv.at[index],
            device_id=device((shift, 0, 0)), device_id_type=MESH,
        )

    for index, shift in enumerate(plan.moves):
        low, high = plan.shifts[shift]
        for a, ref in enumerate((init_ref, source_ref)):
            @pl.loop(low, high)
            def _(r, a=a, ref=ref, index=index, shift=shift):
                move_out[index, a, r] = pick(ref, shift, r)

        @pl.when(has[shift, 0, 0])
        def _(index=index, shift=shift):
            move_of(index, shift).start()

    slot_q = plan.bases[2]
    for a, ref in enumerate((init_ref, source_ref)):
        @pl.loop(0, cx)
        def _(r, a=a, ref=ref):
            send[slot_q + a, r] = pick(ref, 0, r)

    row = lax.broadcasted_iota(jnp.int32, (ext_y, cz), 0)
    col = lax.broadcasted_iota(jnp.int32, (ext_y, cz), 1)
    in_rows = (row < cy) | ((row < cy + WIDE) & has[0, 1, 0]) | ((row >= ext_y - WIDE) & has[0, -1, 0])
    in_cols = ((col < WIDE) & has[0, 0, 1]) | ((col >= cz - WIDE) & has[0, 0, -1])
    maskv[0] = jnp.where(in_rows, 1.0, 0.0)
    maskv[1] = jnp.where(in_rows & in_cols, 1.0, 0.0)

    for k in range(cx):
        value = send[0, k]
        resid[0, WIDE + k, 0:cy] = value
        dir_a[0, WIDE + k, 0:cy] = value * (1.0 / THETA)
        field_ref[k] = value * (1.0 / THETA)
        kap[0, WIDE + k, 0:cy] = send[1, k] + 6.0

    first_col, last_col = col == 0, col == cz - 1

    def sides(ref, e):
        core, outer = ref[0, e], ref[1, e]
        core_r, outer_r = pltpu.roll(core, cz - 1, 1), pltpu.roll(outer, cz - 1, 1)
        core_l, outer_l = pltpu.roll(core, 1, 1), pltpu.roll(outer, 1, 1)
        return (
            (core, pltpu.roll(core, 1, 0), pltpu.roll(core, ext_y - 1, 0),
             jnp.where(first_col, outer_l, core_l), jnp.where(last_col, outer_r, core_r)),
            (outer, pltpu.roll(outer, 1, 0), pltpu.roll(outer, ext_y - 1, 0),
             jnp.where(first_col, core_l, outer_l), jnp.where(last_col, core_r, outer_r)),
        )

    weights = sweep_weights(SWEEPS)

    def inside(e):
        at = me[0] * cx - WIDE + e
        return (at >= 0) & (at < plan.size[0] * cx)

    def planes_of(low, high):
        for first, end, own in ((0, WIDE, False), (WIDE, WIDE + cx, True), (WIDE + cx, ext_x, False)):
            first, end = max(first, low), min(end, high)
            if first < end:
                yield first, end, own

    def parts(step, width, beside):
        low, high = WIDE - width + step + 1, WIDE + cx + width - step - 1
        inner_low, inner_high = WIDE + 1 + step, WIDE + cx - 1 - step
        inner_low = min(inner_low, inner_high)
        if beside:
            return [(inner_low, inner_high)]
        return [(low, inner_low), (inner_high, high)]

    def cheb_wide(old, new, weight, low, high):
        for first, end, own in planes_of(low, high):
            @pl.loop(first, end, unroll=True)
            def _(e, own=own):
                okay = jnp.where(inside(e), 1.0, 0.0)
                for zt, (mid, up, down, left, right) in enumerate(sides(old, e)):
                    beside = old[zt, e - 1] + old[zt, e + 1] + (up + down) + (left + right)
                    part = maskv[zt] if own else maskv[zt] * okay
                    rest = resid[zt, e] - (kap[zt, e] * mid - beside) * part
                    resid[zt, e] = rest
                    value = weight[0] * mid + weight[1] * rest
                    new[zt, e] = value
                    if own and zt == 0:
                        field_ref[e - WIDE] = field_ref[e - WIDE] + value[0:cy]

    def cheb_core(old, new, weight, slot, low, high):
        @pl.loop(low, high, unroll=True)
        def _(e):
            k = e - WIDE
            mid, up, down, left, right = sides(old, e)[0]
            beside = old[0, e - 1] + old[0, e + 1] + (up + down) + (left + right)
            rest = (resid[0, e] - (kap[0, e] * mid - beside))[0:cy]
            value = weight[0] * mid[0:cy] + weight[1] * rest
            total = field_ref[k] + value
            field_ref[k] = total
            if slot is None:
                raised = jnp.exp(LOG_GAIN * total)
                send[plan.bases[3], k] = raised
                perm[0, e, 0:cy] = raised
            else:
                resid[0, e, 0:cy] = rest
                new[0, e, 0:cy] = value
                send[slot, k] = value
                send[slot + 1, k] = rest

    def cheb_block(beside, first, count, slot):
        for step in range(count):
            for low, high in parts(step, count, beside):
                if low >= high:
                    continue
                weight = weights[first + step]
                if step < count - 1:
                    cheb_wide(dir_l[step], dir_l[step + 1], weight, low, high)
                else:
                    cheb_core(dir_l[step], dir_a, weight, slot, low, high)

    def put_noise(zt, e, r, value):
        resid[zt, e, r : r + 8] = value
        dir_a[zt, e, r : r + 8] = value * (1.0 / THETA)

    def put_kappa(zt, e, r, value):
        kap[zt, e, r : r + 8] = value + 6.0

    for beside in (True, False):
        finish(0, beside)
        assemble(0, 0, put_noise, beside)
        assemble(0, 1, put_kappa, beside)
        cheb_block(beside, 0, 4, plan.bases[1])
    start(1)

    for index, shift in enumerate(plan.moves):
        low, high = plan.shifts[shift]

        @pl.when(has[-shift, 0, 0])
        def _(index=index, shift=shift, low=low, high=high):
            move_of(index, shift).wait_recv()
            for a in range(2):
                send[slot_q + a, low:high] = send[slot_q + a, low:high] + move_in[index, a, low:high]

        @pl.when(has[shift, 0, 0])
        def _(index=index, shift=shift):
            move_of(index, shift).wait_send()

    start(2)

    def put_dir(zt, e, r, value):
        dir_a[zt, e, r : r + 8] = value

    def put_resid(zt, e, r, value):
        resid[zt, e, r : r + 8] = value

    for beside in (True, False):
        finish(1, beside)
        assemble(1, 0, put_dir, beside)
        assemble(1, 1, put_resid, beside)
        cheb_block(beside, 4, 3, None)
    start(3)


    def put_init(zt, e, r, value):
        prs_a[zt, e, r : r + 8] = value

    def put_charge(zt, e, r, value):
        charge[zt, e, r : r + 8] = value

    for beside in (True, False):
        finish(2, beside)
        assemble(2, 0, put_init, beside)
        assemble(2, 1, put_charge, beside)
    for k in range(cx):
        prs_a[0, WIDE + k, 0:cy] = send[slot_q, k]
        charge[0, WIDE + k, 0:cy] = send[slot_q + 1, k]


    def put_perm(zt, e, r, value):
        perm[zt, e, r : r + 8] = value


    top = (row == 0) & (me[1] == 0)
    bottom = (row == cy - 1) & (me[1] == plan.size[1] - 1)
    near = first_col & (me[2] == 0)
    far = last_col & (me[2] == plan.size[2] - 1)

    def harmonic(own, other):
        return 2.0 * own * other / (own + other)

    def couple_x(e):
        plane = me[0] * cx - WIDE + e - inset_begin
        pair = (plane >= 0) & (plane < plan.inset - 1)
        for zt in range(2):
            coef[0, zt, e] = jnp.where(pair, harmonic(perm[zt, e], perm[zt, e + 1]), 0.0)

    def couple(e):
        plane = me[0] * cx - WIDE + e - inset_begin
        okay = (plane >= 0) & (plane < plan.inset)
        (core, _, core_down, _, core_right), (outer, _, outer_down, _, outer_right) = sides(perm, e)
        core_z = jnp.where(okay, harmonic(core, core_right), 0.0)
        outer_z = jnp.where(okay, harmonic(outer, outer_right), 0.0)
        core_back, outer_back = pltpu.roll(core_z, 1, 1), pltpu.roll(outer_z, 1, 1)
        core_left = jnp.where(first_col, outer_back, core_back)
        outer_left = jnp.where(first_col, core_back, outer_back)
        core_left, core_fore = jnp.where(near, core, core_left), jnp.where(far, core, core_z)
        for zt, mid, down, z_left, z_right, z_pair in (
            (0, core, core_down, core_left, core_fore, core_z),
            (1, outer, outer_down, outer_left, outer_z, outer_z),
        ):
            below = jnp.where(plane == 0, mid, coef[0, zt, e - 1])
            above = jnp.where(plane == plan.inset - 1, mid, coef[0, zt, e])
            y_pair = jnp.where(okay, harmonic(mid, down), 0.0)
            y_up = jnp.where(top, mid, pltpu.roll(y_pair, 1, 0))
            y_down = jnp.where(bottom, mid, y_pair)
            total = below + above + y_up + y_down + z_left + z_right
            valid = (maskv[zt] > 0.5) & okay
            coef[1, zt, e] = y_pair
            coef[2, zt, e] = z_pair
            coef[3, zt, e] = jnp.where(valid, 1.0 / total, 0.0)

    def flux(old, e, outer_too):
        core, outer = old[0, e], old[1, e]
        core_z, outer_z = coef[2, 0, e], coef[2, 1, e]
        core_r, outer_r = pltpu.roll(core, cz - 1, 1), pltpu.roll(outer, cz - 1, 1)
        core_l, outer_l = pltpu.roll(core * core_z, 1, 1), pltpu.roll(outer * outer_z, 1, 1)
        along = [jnp.where(last_col, outer_r, core_r) * core_z + jnp.where(first_col, outer_l, core_l)]
        if outer_too:
            along.append(jnp.where(last_col, core_r, outer_r) * outer_z + jnp.where(first_col, core_l, outer_l))
        values = []
        for zt, value in enumerate(along):
            mid, y_pair = (core, outer)[zt], coef[1, zt, e]
            value = value + charge[zt, e]
            value = value + (coef[0, zt, e - 1] * old[zt, e - 1] + coef[0, zt, e] * old[zt, e + 1])
            value = value + (y_pair * pltpu.roll(mid, ext_y - 1, 0) + pltpu.roll(y_pair * mid, 1, 0))
            values.append(value * coef[3, zt, e])
        return values

    def jacobi_wide(old, new, low, high):
        @pl.loop(low, high, unroll=True)
        def _(e):
            for zt, value in enumerate(flux(old, e, True)):
                new[zt, e] = value

    def jacobi_core(old, new, slot, low, high):
        @pl.loop(low, high, unroll=True)
        def _(e):
            k = e - WIDE
            value = flux(old, e, False)[0][0:cy]
            if slot is None:
                last[k] = value
            else:
                new[0, e, 0:cy] = value
                send[slot, k] = value

    def jacobi_block(beside, count, slot):
        for step in range(count):
            for low, high in parts(step, count, beside):
                if low >= high:
                    continue
                if step < count - 1:
                    jacobi_wide(prs_l[step], prs_l[step + 1], low, high)
                else:
                    jacobi_core(prs_l[step], prs_a, slot, low, high)

    def over(ranges, body):
        for low, high in ranges:
            pl.loop(low, high, unroll=True)(body)

    inner, end = WIDE + cx - 1, ext_x - 1
    for beside in (True, False):
        finish(3, beside)
        assemble(3, 0, put_perm, beside, fill=1.0)
        over([(WIDE, inner)] if beside else [(0, WIDE), (inner, end)], couple_x)
        over([(WIDE + 1, inner)] if beside else [(1, WIDE + 1), (inner, end)], couple)
        jacobi_block(beside, 4, plan.bases[4])
    start(4)
    for beside in (True, False):
        finish(4, beside)
        assemble(4, 0, put_init, beside)
        jacobi_block(beside, 4, None)

    def last_of(index, shift):
        low, high = plan.shifts[shift]
        at = (shift - plan.lowest) * cx + low
        return pltpu.make_async_remote_copy(
            src_ref=last.at[pl.ds(low, high - low)],
            dst_ref=landed.at[pl.ds(at, high - low)],
            send_sem=last_send.at[index], recv_sem=last_recv.at[index],
            device_id=device((-shift, 0, 0)), device_id_type=MESH,
        )

    for index, shift in enumerate(plan.moves):
        @pl.when(has[-shift, 0, 0])
        def _(index=index, shift=shift):
            last_of(index, shift).start()

    landed[-plan.lowest * cx : (1 - plan.lowest) * cx] = last[...]
    for index, shift in enumerate(plan.moves):
        @pl.when(has[shift, 0, 0])
        def _(index=index, shift=shift):
            last_of(index, shift).wait_recv()

    window = (plan.highest - plan.lowest + 1) * cx

    @pl.loop(0, plan.flow_rows)
    def _(j):
        at = inset_begin + cut_here + j - cx * (me[0] + plan.lowest)
        value = landed[jnp.clip(at, 0, window - 1)]
        pressure_ref[j] = jnp.where(j < count_here, value, 0.0)

    for index, shift in enumerate(plan.moves):
        @pl.when(has[-shift, 0, 0])
        def _(index=index, shift=shift):
            last_of(index, shift).wait_send()

    for rnd in range(len(plan.rounds)):
        let_go(rnd)


def local(mesh, noise, kappa_sq, cuts, pressure_init, source):
    cells, flow_rows = noise.shape, pressure_init.shape[0]
    plan = Plan(mesh, cells, flow_rows)
    cx, cy, cz = cells
    block = (2, cx + 2 * WIDE, cy + 8, cz)
    moves = max(1, len(plan.moves))
    f32 = jnp.float32
    vmem = lambda *shape: pltpu.VMEM(shape, f32)
    sems = lambda *shape: pltpu.SemaphoreType.DMA(shape)
    total = plan.total
    return pl.pallas_call(
        functools.partial(kernel, plan),
        out_shape=(
            jax.ShapeDtypeStruct(noise.shape, f32),
            jax.ShapeDtypeStruct(pressure_init.shape, f32),
        ),
        in_specs=[pl.BlockSpec(memory_space=pl.ANY)] * 5,
        out_specs=(pl.BlockSpec(memory_space=pltpu.VMEM),) * 2,
        scratch_shapes=[
            vmem(4, *block), vmem(*block), vmem(*block), vmem(4, *block),
            vmem(4, *block), vmem(*block), vmem(*block), vmem(2, cy + 8, cz),
            vmem(*pressure_init.shape), vmem(*source.shape),
            pltpu.SMEM(cuts.shape, jnp.int32), sems(5),
            vmem(total, cx, cy, cz), vmem(2, total, 8, cz),
            vmem(2, total, WIDE, cy, cz), vmem(2, total, cx, 8, cz),
            vmem(2, 2, total, WIDE, 8, cz), vmem(3, 3, 2, total, 8, cz),
            vmem(moves, 2, cx, cy, cz), vmem(moves, 2, cx, cy, cz),
            vmem(cx, cy, cz), vmem((plan.highest - plan.lowest + 1) * cx, cy, cz),
            sems(len(plan.rounds), len(OFFSETS) + 2), sems(len(plan.rounds), len(OFFSETS) + 2),
            sems(moves), sems(moves), sems(moves), sems(moves),
        ],
        compiler_params=pltpu.CompilerParams(
            collective_id=0, has_side_effects=True, vmem_limit_bytes=64 * 1024 * 1024
        ),
        cost_estimate=pl.CostEstimate(flops=30_000_000, bytes_accessed=1_000_000, transcendentals=32768),
        name="sweeps",
    )(cuts, noise, kappa_sq, pressure_init, source)


def solution(mesh):
    part = P("gx", "gy", "gz")
    return jax.shard_map(
        functools.partial(local, mesh),
        mesh=mesh,
        in_specs=(part, part, P(), part, part),
        out_specs=(part, part),
        check_vma=False,
    )
```

```python
import functools

import jax
import jax.numpy as jnp
from jax import lax
from jax.experimental import pallas as pl
from jax.experimental.pallas import tpu as pltpu
from jax.sharding import PartitionSpec as P

SWEEPS = 8
JACOBI = 8
THETA = 7.125
DELTA = 6.875
LOG_GAIN = 2.0
WIDE = 4
MESH = pl.DeviceIdType.MESH

OFFSETS = [
    (x, y, z)
    for x in (-1, 0, 1)
    for y in (-1, 0, 1)
    for z in (-1, 0, 1)
    if abs(x) + abs(y) + abs(z) >= 1
]
OFFSETS.sort(key=lambda o: (o[2] != 0, abs(o[0]) + abs(o[1]) + abs(o[2]), -abs(o[0])))


def sweep_weights(count):
    ratio_base = THETA / DELTA
    ratio_now = 1.0 / ratio_base
    weights = []
    for index in range(count):
        ratio_next = 1.0 / (2.0 * ratio_base - ratio_now)
        weights.append((ratio_next * ratio_now, 2.0 * ratio_next / DELTA))
        ratio_now = ratio_next
    return weights


class Plan:
    def __init__(self, mesh, cells, flow_rows):
        self.size = (mesh.shape["gx"], mesh.shape["gy"], mesh.shape["gz"])
        self.cells = cells
        self.flow_rows = flow_rows
        self.inset = 3 * cells[0] * self.size[0] // 4
        cx, count = cells[0], self.size[0]
        mean = 3 * cx // 4
        jitter = (mean - 2) // 2
        centre = cx * count // 8
        self.shifts = {}
        for shift in range(1 - count, count):
            low, high = cx, 0
            for tile in range(max(0, -shift), min(count, count - shift)):
                begin = mean * tile + centre - 2 * jitter - cx * (tile + shift)
                end = begin + flow_rows + 2 * jitter
                if max(begin, 0) < min(end, cx):
                    low, high = min(low, max(begin, 0)), max(high, min(end, cx))
            if low < high:
                self.shifts[shift] = (low, high)
        self.shifts[0] = (0, cx)
        self.lowest, self.highest = min(self.shifts), max(self.shifts)
        self.moves = [s for s in sorted(self.shifts, key=abs) if s != 0]
        self.rounds = [(2, 4), (2, 3), (2, 4), (1, 4), (1, 4)]
        self.bases = [sum(n for n, _ in self.rounds[:i]) for i in range(len(self.rounds))]
        self.total = sum(n for n, _ in self.rounds)


def kernel(
    plan,
    cuts_hbm, noise_hbm, kappa_hbm, init_hbm, source_hbm,
    field_ref, pressure_ref,
    dirs, resid, kap, press, coef, charge, perm, maskv,
    init_in, source_in, cuts_in, load_sem,
    send, packed, land_x, land_y, land_xy, land_p,
    move_out, move_in, last, landed,
    send_sem, recv_sem, move_send, move_recv, last_send, last_recv,
):
    cx, cy, cz = plan.cells
    ext_x, ext_y = cx + 2 * WIDE, cy + 8
    me = [lax.axis_index("gx"), lax.axis_index("gy"), lax.axis_index("gz")]
    tiles_y = cy // 8

    def there(offset):
        flag = None
        for at, by, size in zip(me, offset, plan.size):
            if by == 0:
                continue
            one = (at + by < size) if by > 0 else (at + by >= 0)
            flag = one if flag is None else flag & one
        return flag

    def device(offset):
        return tuple(at + by for at, by in zip(me, offset))

    has = {o: there(o) for o in OFFSETS}
    greet = [o for o in OFFSETS] + [(s, 0, 0) for s in plan.moves if abs(s) > 1]
    for s in plan.moves:
        has[(s, 0, 0)] = there((s, 0, 0))
        has[(-s, 0, 0)] = there((-s, 0, 0))

    init_ref, source_ref, cuts_ref = init_in, source_in, cuts_in
    loads = [
        pltpu.make_async_copy(noise_hbm, send.at[0], load_sem.at[0]),
        pltpu.make_async_copy(kappa_hbm, send.at[1], load_sem.at[1]),
        pltpu.make_async_copy(init_hbm, init_in, load_sem.at[2]),
        pltpu.make_async_copy(source_hbm, source_in, load_sem.at[3]),
        pltpu.make_async_copy(cuts_hbm, cuts_in, load_sem.at[4]),
    ]
    for load in loads:
        load.start()

    barrier = pltpu.get_barrier_semaphore()
    expected = jnp.int32(0)
    for o in greet:
        expected = expected + has[o].astype(jnp.int32)

        @pl.when(has[o])
        def _(o=o):
            pl.semaphore_signal(barrier, inc=1, device_id=device(o), device_id_type=MESH)


    dir_l, prs_l = [dirs.at[i] for i in range(4)], [press.at[i] for i in range(4)]
    dir_a, prs_a = dir_l[0], prs_l[0]
    lane = lax.broadcasted_iota(jnp.int32, (8, cz), 1)
    row8 = lax.broadcasted_iota(jnp.int32, (8, cz), 0)

    def offsets_of(width):
        return [(i, o) for i, o in enumerate(OFFSETS) if sum(map(abs, o)) <= width]

    def copies_of(rnd):
        n, w = plan.rounds[rnd]
        listed = [(i, o, 0) for i, o in offsets_of(w)]
        if n > 1:
            extra = [o for o in OFFSETS if o[1] == 0 and o[2] == 0]
            listed = [(len(OFFSETS) + i, o, 1) for i, o in enumerate(extra)] + listed
        return sorted(listed, key=lambda c: (c[1][2] != 0, c[1][0] == 0 or c[1][1] != 0, c[2]))

    def copy_of(rnd, index, o, a):
        n, w = plan.rounds[rnd]
        arrays = pl.ds(plan.bases[rnd], n)
        if o[0] != 0 and o[1] == 0 and o[2] == 0:
            w, arrays = w - a, pl.ds(plan.bases[rnd] + a, 1)
        planes = {0: pl.ds(0, cx), 1: pl.ds(cx - w, w), -1: pl.ds(0, w)}[o[0]]
        rows = {0: pl.ds(0, cy), 1: pl.ds(cy - 8, 8), -1: pl.ds(0, 8)}[o[1]]
        fx, fy = (0 if o[0] > 0 else 1), (0 if o[1] > 0 else 1)
        if o[2] != 0:
            side = 0 if o[2] < 0 else 1
            src = packed.at[side, arrays]
            dst = land_p.at[1 - o[0], 1 - o[1], side, arrays]
        elif o[0] != 0 and o[1] != 0:
            src = send.at[arrays, planes, rows]
            dst = land_xy.at[fx, fy, arrays, pl.ds(0, w)]
        elif o[0] != 0:
            src = send.at[arrays, planes, rows]
            dst = land_x.at[fx, arrays, pl.ds(0, w)]
        else:
            src = send.at[arrays, planes, rows]
            dst = land_y.at[fy, arrays]
        return pltpu.make_async_remote_copy(
            src_ref=src, dst_ref=dst,
            send_sem=send_sem.at[rnd, index], recv_sem=recv_sem.at[rnd, index],
            device_id=device(o), device_id_type=MESH,
        )

    def issue(rnd, chosen):
        for index, o, a in copies_of(rnd):
            if chosen(o):
                @pl.when(has[o])
                def _(index=index, o=o, a=a):
                    copy_of(rnd, index, o, a).start()

    def pack(rnd):
        n, w = plan.rounds[rnd]
        for a in range(n):
            slot = plan.bases[rnd] + a
            low = high = None
            for k in range(cx):
                for j in range(tiles_y):
                    by = (j * cx + k) * w
                    value = send[slot, k, 8 * j : 8 * j + 8]
                    to_low = jnp.where(lane < w, value, 0.0)
                    to_high = jnp.where(lane >= cz - w, value, 0.0)
                    if by:
                        to_low = low + pltpu.roll(to_low, by, 1)
                        to_high = high + pltpu.roll(to_high, cz - by, 1)
                    low, high = to_low, to_high
            packed[0, slot] = low
            packed[1, slot] = high

    def start(rnd, ready=False):
        issue(rnd, lambda o: o[0] == 0 and o[2] == 0)
        if not ready:
            pack(rnd)
        issue(rnd, lambda o: o[0] == 0 and o[2] != 0)
        issue(rnd, lambda o: o[0] != 0 and o[2] == 0)
        issue(rnd, lambda o: o[0] != 0 and o[2] != 0)

    def finish(rnd, beside):
        for index, o, a in copies_of(rnd):
            if (o[0] == 0) == beside:
                @pl.when(has[tuple(-v for v in o)])
                def _(index=index, o=o, a=a):
                    copy_of(rnd, index, o, a).wait_recv()

    def let_go(rnd):
        for index, o, a in copies_of(rnd):
            @pl.when(has[o])
            def _(index=index, o=o, a=a):
                copy_of(rnd, index, o, a).wait_send()

    def assemble(rnd, a, put, beside, fill=0.0):
        n, w = plan.rounds[rnd]
        slot = plan.bases[rnd] + a
        blank = jnp.full((8, cz), fill, jnp.float32)
        arrived = {}
        for o in OFFSETS:
            if o[2] != 0 and sum(map(abs, o)) <= w and (o[0] == 0) == beside:
                side = 0 if o[2] > 0 else 1
                arrived[o] = jnp.where(has[o], land_p[1 + o[0], 1 + o[1], side, slot], blank)

        def unpack(dx, dy, k, j):
            by = (j * cx + k) * w
            value = blank
            if (dx, dy, 1) in arrived:
                right = pltpu.roll(arrived[dx, dy, 1], (cz - by) % cz, 1)
                value = jnp.where(lane < w, right, value)
                left = pltpu.roll(arrived[dx, dy, -1], by, 1)
                value = jnp.where(lane >= cz - w, left, value)
            return value

        def between(after, before):
            return jnp.where(row8 < w, after, jnp.where(row8 >= 8 - w, before, blank))

        def columns(dx, k, plane):
            for j in range(tiles_y):
                put(1, plane, 8 * j, unpack(dx, 0, k, j))
            put(1, plane, cy, between(unpack(dx, 1, k, 0), unpack(dx, -1, k, tiles_y - 1)))

        for k in range(cx) if beside else ():
            after = jnp.where(has[0, 1, 0], land_y[1, slot, k], blank)
            before = jnp.where(has[0, -1, 0], land_y[0, slot, k], blank)
            put(0, WIDE + k, cy, between(after, before))
            columns(0, k, WIDE + k)
        wide = w - a
        for dx in () if beside else (-1, 1):
            fx = 0 if dx < 0 else 1
            for q in range(wide):
                plane = WIDE - wide + q if dx < 0 else WIDE + cx + q
                k = cx - wide + q if dx < 0 else q
                i = q + a if dx < 0 else q
                big = jnp.where(has[dx, 0, 0], land_x[fx, slot, q], jnp.full((cy, cz), fill, jnp.float32))
                for j in range(tiles_y):
                    put(0, plane, 8 * j, big[8 * j : 8 * j + 8])
                after = jnp.where(has[dx, 1, 0], land_xy[fx, 1, slot, i], blank)
                before = jnp.where(has[dx, -1, 0], land_xy[fx, 0, slot, i], blank)
                put(0, plane, cy, between(after, before))
                columns(dx, k, plane)

    loads[0].wait()
    loads[1].wait()
    pack(0)
    pl.semaphore_wait(barrier, expected)
    start(0, ready=True)
    for load in loads[2:]:
        load.wait()

    inset_begin = cuts_ref[0]
    cut_here = cuts_ref[me[0] + 1]
    count_here = cuts_ref[me[0] + 2] - cut_here

    def pick(ref, shift, r):
        row = cx * (me[0] + shift) + r - inset_begin - cut_here
        value = ref[jnp.clip(row, 0, plan.flow_rows - 1)]
        return jnp.where((row >= 0) & (row < count_here), value, 0.0)

    def move_of(index, shift):
        low, high = plan.shifts[shift]
        return pltpu.make_async_remote_copy(
            src_ref=move_out.at[index, :, pl.ds(low, high - low)],
            dst_ref=move_in.at[index, :, pl.ds(low, high - low)],
            send_sem=move_send.at[index], recv_sem=move_recv.at[index],
            device_id=device((shift, 0, 0)), device_id_type=MESH,
        )

    for index, shift in enumerate(plan.moves):
        low, high = plan.shifts[shift]
        for a, ref in enumerate((init_ref, source_ref)):
            @pl.loop(low, high)
            def _(r, a=a, ref=ref, index=index, shift=shift):
                move_out[index, a, r] = pick(ref, shift, r)

        @pl.when(has[shift, 0, 0])
        def _(index=index, shift=shift):
            move_of(index, shift).start()

    slot_q = plan.bases[2]
    for a, ref in enumerate((init_ref, source_ref)):
        @pl.loop(0, cx)
        def _(r, a=a, ref=ref):
            send[slot_q + a, r] = pick(ref, 0, r)

    row = lax.broadcasted_iota(jnp.int32, (ext_y, cz), 0)
    col = lax.broadcasted_iota(jnp.int32, (ext_y, cz), 1)
    in_rows = (row < cy) | ((row < cy + WIDE) & has[0, 1, 0]) | ((row >= ext_y - WIDE) & has[0, -1, 0])
    in_cols = ((col < WIDE) & has[0, 0, 1]) | ((col >= cz - WIDE) & has[0, 0, -1])
    maskv[0] = jnp.where(in_rows, 1.0, 0.0)
    maskv[1] = jnp.where(in_rows & in_cols, 1.0, 0.0)

    for k in range(cx):
        value = send[0, k]
        resid[0, WIDE + k, 0:cy] = value
        dir_a[0, WIDE + k, 0:cy] = value * (1.0 / THETA)
        field_ref[k] = value * (1.0 / THETA)
        kap[0, WIDE + k, 0:cy] = send[1, k] + 6.0

    first_col, last_col = col == 0, col == cz - 1

    def sides(ref, e):
        core, outer = ref[0, e], ref[1, e]
        core_r, outer_r = pltpu.roll(core, cz - 1, 1), pltpu.roll(outer, cz - 1, 1)
        core_l, outer_l = pltpu.roll(core, 1, 1), pltpu.roll(outer, 1, 1)
        return (
            (core, pltpu.roll(core, 1, 0), pltpu.roll(core, ext_y - 1, 0),
             jnp.where(first_col, outer_l, core_l), jnp.where(last_col, outer_r, core_r)),
            (outer, pltpu.roll(outer, 1, 0), pltpu.roll(outer, ext_y - 1, 0),
             jnp.where(first_col, core_l, outer_l), jnp.where(last_col, core_r, outer_r)),
        )

    weights = sweep_weights(SWEEPS)

    def inside(e):
        at = me[0] * cx - WIDE + e
        return (at >= 0) & (at < plan.size[0] * cx)

    def planes_of(low, high):
        for first, end, own in ((0, WIDE, False), (WIDE, WIDE + cx, True), (WIDE + cx, ext_x, False)):
            first, end = max(first, low), min(end, high)
            if first < end:
                yield first, end, own

    def parts(step, width, beside):
        low, high = WIDE - width + step + 1, WIDE + cx + width - step - 1
        inner_low, inner_high = WIDE + 1 + step, WIDE + cx - 1 - step
        inner_low = min(inner_low, inner_high)
        if beside:
            return [(inner_low, inner_high)]
        return [(low, inner_low), (inner_high, high)]

    def cheb_wide(old, new, weight, low, high):
        for first, end, own in planes_of(low, high):
            @pl.loop(first, end, unroll=True)
            def _(e, own=own):
                okay = jnp.where(inside(e), 1.0, 0.0)
                for zt, (mid, up, down, left, right) in enumerate(sides(old, e)):
                    beside = old[zt, e - 1] + old[zt, e + 1] + (up + down) + (left + right)
                    part = maskv[zt] if own else maskv[zt] * okay
                    rest = resid[zt, e] - (kap[zt, e] * mid - beside) * part
                    resid[zt, e] = rest
                    value = weight[0] * mid + weight[1] * rest
                    new[zt, e] = value
                    if own and zt == 0:
                        field_ref[e - WIDE] = field_ref[e - WIDE] + value[0:cy]

    def cheb_core(old, new, weight, slot, low, high):
        @pl.loop(low, high, unroll=True)
        def _(e):
            k = e - WIDE
            mid, up, down, left, right = sides(old, e)[0]
            beside = old[0, e - 1] + old[0, e + 1] + (up + down) + (left + right)
            rest = (resid[0, e] - (kap[0, e] * mid - beside))[0:cy]
            value = weight[0] * mid[0:cy] + weight[1] * rest
            total = field_ref[k] + value
            field_ref[k] = total
            if slot is None:
                raised = jnp.exp(LOG_GAIN * total)
                send[plan.bases[3], k] = raised
                perm[0, e, 0:cy] = raised
            else:
                resid[0, e, 0:cy] = rest
                new[0, e, 0:cy] = value
                send[slot, k] = value
                send[slot + 1, k] = rest

    def cheb_block(beside, first, count, slot):
        for step in range(count):
            for low, high in parts(step, count, beside):
                if low >= high:
                    continue
                weight = weights[first + step]
                if step < count - 1:
                    cheb_wide(dir_l[step], dir_l[step + 1], weight, low, high)
                else:
                    cheb_core(dir_l[step], dir_a, weight, slot, low, high)

    def put_noise(zt, e, r, value):
        resid[zt, e, r : r + 8] = value
        dir_a[zt, e, r : r + 8] = value * (1.0 / THETA)

    def put_kappa(zt, e, r, value):
        kap[zt, e, r : r + 8] = value + 6.0

    for beside in (True, False):
        finish(0, beside)
        assemble(0, 0, put_noise, beside)
        assemble(0, 1, put_kappa, beside)
        cheb_block(beside, 0, 4, plan.bases[1])
    start(1)

    for index, shift in enumerate(plan.moves):
        low, high = plan.shifts[shift]

        @pl.when(has[-shift, 0, 0])
        def _(index=index, shift=shift, low=low, high=high):
            move_of(index, shift).wait_recv()
            for a in range(2):
                send[slot_q + a, low:high] = send[slot_q + a, low:high] + move_in[index, a, low:high]

        @pl.when(has[shift, 0, 0])
        def _(index=index, shift=shift):
            move_of(index, shift).wait_send()

    start(2)

    def put_dir(zt, e, r, value):
        dir_a[zt, e, r : r + 8] = value

    def put_resid(zt, e, r, value):
        resid[zt, e, r : r + 8] = value

    for beside in (True, False):
        finish(1, beside)
        assemble(1, 0, put_dir, beside)
        assemble(1, 1, put_resid, beside)
        cheb_block(beside, 4, 3, None)
    start(3)


    def put_init(zt, e, r, value):
        prs_a[zt, e, r : r + 8] = value

    def put_charge(zt, e, r, value):
        charge[zt, e, r : r + 8] = value

    for beside in (True, False):
        finish(2, beside)
        assemble(2, 0, put_init, beside)
        assemble(2, 1, put_charge, beside)
    for k in range(cx):
        prs_a[0, WIDE + k, 0:cy] = send[slot_q, k]
        charge[0, WIDE + k, 0:cy] = send[slot_q + 1, k]


    def put_perm(zt, e, r, value):
        perm[zt, e, r : r + 8] = value


    top = (row == 0) & (me[1] == 0)
    bottom = (row == cy - 1) & (me[1] == plan.size[1] - 1)
    near = first_col & (me[2] == 0)
    far = last_col & (me[2] == plan.size[2] - 1)

    def harmonic(own, other):
        return 2.0 * own * other / (own + other)

    def couple_x(e):
        plane = me[0] * cx - WIDE + e - inset_begin
        pair = (plane >= 0) & (plane < plan.inset - 1)
        for zt in range(2):
            coef[0, zt, e] = jnp.where(pair, harmonic(perm[zt, e], perm[zt, e + 1]), 0.0)

    def couple(e):
        plane = me[0] * cx - WIDE + e - inset_begin
        okay = (plane >= 0) & (plane < plan.inset)
        (core, _, core_down, _, core_right), (outer, _, outer_down, _, outer_right) = sides(perm, e)
        core_z = jnp.where(okay, harmonic(core, core_right), 0.0)
        outer_z = jnp.where(okay, harmonic(outer, outer_right), 0.0)
        core_back, outer_back = pltpu.roll(core_z, 1, 1), pltpu.roll(outer_z, 1, 1)
        core_left = jnp.where(first_col, outer_back, core_back)
        outer_left = jnp.where(first_col, core_back, outer_back)
        core_left, core_fore = jnp.where(near, core, core_left), jnp.where(far, core, core_z)
        for zt, mid, down, z_left, z_right, z_pair in (
            (0, core, core_down, core_left, core_fore, core_z),
            (1, outer, outer_down, outer_left, outer_z, outer_z),
        ):
            below = jnp.where(plane == 0, mid, coef[0, zt, e - 1])
            above = jnp.where(plane == plan.inset - 1, mid, coef[0, zt, e])
            y_pair = jnp.where(okay, harmonic(mid, down), 0.0)
            y_up = jnp.where(top, mid, pltpu.roll(y_pair, 1, 0))
            y_down = jnp.where(bottom, mid, y_pair)
            total = below + above + y_up + y_down + z_left + z_right
            valid = (maskv[zt] > 0.5) & okay
            coef[1, zt, e] = y_pair
            coef[2, zt, e] = z_pair
            coef[3, zt, e] = jnp.where(valid, 1.0 / total, 0.0)

    def flux(old, e, outer_too):
        core, outer = old[0, e], old[1, e]
        core_z, outer_z = coef[2, 0, e], coef[2, 1, e]
        core_r, outer_r = pltpu.roll(core, cz - 1, 1), pltpu.roll(outer, cz - 1, 1)
        core_l, outer_l = pltpu.roll(core * core_z, 1, 1), pltpu.roll(outer * outer_z, 1, 1)
        along = [jnp.where(last_col, outer_r, core_r) * core_z + jnp.where(first_col, outer_l, core_l)]
        if outer_too:
            along.append(jnp.where(last_col, core_r, outer_r) * outer_z + jnp.where(first_col, core_l, outer_l))
        values = []
        for zt, value in enumerate(along):
            mid, y_pair = (core, outer)[zt], coef[1, zt, e]
            value = value + charge[zt, e]
            value = value + (coef[0, zt, e - 1] * old[zt, e - 1] + coef[0, zt, e] * old[zt, e + 1])
            value = value + (y_pair * pltpu.roll(mid, ext_y - 1, 0) + pltpu.roll(y_pair * mid, 1, 0))
            values.append(value * coef[3, zt, e])
        return values

    def jacobi_wide(old, new, low, high):
        @pl.loop(low, high, unroll=True)
        def _(e):
            for zt, value in enumerate(flux(old, e, True)):
                new[zt, e] = value

    def jacobi_core(old, new, slot, low, high):
        @pl.loop(low, high, unroll=True)
        def _(e):
            k = e - WIDE
            value = flux(old, e, False)[0][0:cy]
            if slot is None:
                last[k] = value
            else:
                new[0, e, 0:cy] = value
                send[slot, k] = value

    def jacobi_block(beside, count, slot):
        for step in range(count):
            for low, high in parts(step, count, beside):
                if low >= high:
                    continue
                if step < count - 1:
                    jacobi_wide(prs_l[step], prs_l[step + 1], low, high)
                else:
                    jacobi_core(prs_l[step], prs_a, slot, low, high)

    def over(ranges, body):
        for low, high in ranges:
            pl.loop(low, high, unroll=True)(body)

    inner, end = WIDE + cx - 1, ext_x - 1
    for beside in (True, False):
        finish(3, beside)
        assemble(3, 0, put_perm, beside, fill=1.0)
        over([(WIDE, inner)] if beside else [(0, WIDE), (inner, end)], couple_x)
        over([(WIDE + 1, inner)] if beside else [(1, WIDE + 1), (inner, end)], couple)
        jacobi_block(beside, 4, plan.bases[4])
    start(4)
    for beside in (True, False):
        finish(4, beside)
        assemble(4, 0, put_init, beside)
        jacobi_block(beside, 4, None)

    def last_of(index, shift):
        low, high = plan.shifts[shift]
        at = (shift - plan.lowest) * cx + low
        return pltpu.make_async_remote_copy(
            src_ref=last.at[pl.ds(low, high - low)],
            dst_ref=landed.at[pl.ds(at, high - low)],
            send_sem=last_send.at[index], recv_sem=last_recv.at[index],
            device_id=device((-shift, 0, 0)), device_id_type=MESH,
        )

    for index, shift in enumerate(plan.moves):
        @pl.when(has[-shift, 0, 0])
        def _(index=index, shift=shift):
            last_of(index, shift).start()

    landed[-plan.lowest * cx : (1 - plan.lowest) * cx] = last[...]
    for index, shift in enumerate(plan.moves):
        @pl.when(has[shift, 0, 0])
        def _(index=index, shift=shift):
            last_of(index, shift).wait_recv()

    window = (plan.highest - plan.lowest + 1) * cx

    @pl.loop(0, plan.flow_rows)
    def _(j):
        at = inset_begin + cut_here + j - cx * (me[0] + plan.lowest)
        value = landed[jnp.clip(at, 0, window - 1)]
        pressure_ref[j] = jnp.where(j < count_here, value, 0.0)

    for index, shift in enumerate(plan.moves):
        @pl.when(has[-shift, 0, 0])
        def _(index=index, shift=shift):
            last_of(index, shift).wait_send()

    for rnd in range(len(plan.rounds)):
        let_go(rnd)


def local(mesh, noise, kappa_sq, cuts, pressure_init, source):
    cells, flow_rows = noise.shape, pressure_init.shape[0]
    plan = Plan(mesh, cells, flow_rows)
    cx, cy, cz = cells
    block = (2, cx + 2 * WIDE, cy + 8, cz)
    moves = max(1, len(plan.moves))
    f32 = jnp.float32
    vmem = lambda *shape: pltpu.VMEM(shape, f32)
    sems = lambda *shape: pltpu.SemaphoreType.DMA(shape)
    total = plan.total
    return pl.pallas_call(
        functools.partial(kernel, plan),
        out_shape=(
            jax.ShapeDtypeStruct(noise.shape, f32),
            jax.ShapeDtypeStruct(pressure_init.shape, f32),
        ),
        in_specs=[pl.BlockSpec(memory_space=pl.ANY)] * 5,
        out_specs=(pl.BlockSpec(memory_space=pltpu.VMEM),) * 2,
        scratch_shapes=[
            vmem(4, *block), vmem(*block), vmem(*block), vmem(4, *block),
            vmem(4, *block), vmem(*block), vmem(*block), vmem(2, cy + 8, cz),
            vmem(*pressure_init.shape), vmem(*source.shape),
            pltpu.SMEM(cuts.shape, jnp.int32), sems(5),
            vmem(total, cx, cy, cz), vmem(2, total, 8, cz),
            vmem(2, total, WIDE, cy, cz), vmem(2, total, cx, 8, cz),
            vmem(2, 2, total, WIDE, 8, cz), vmem(3, 3, 2, total, 8, cz),
            vmem(moves, 2, cx, cy, cz), vmem(moves, 2, cx, cy, cz),
            vmem(cx, cy, cz), vmem((plan.highest - plan.lowest + 1) * cx, cy, cz),
            sems(len(plan.rounds), len(OFFSETS) + 2), sems(len(plan.rounds), len(OFFSETS) + 2),
            sems(moves), sems(moves), sems(moves), sems(moves),
        ],
        compiler_params=pltpu.CompilerParams(
            collective_id=0, has_side_effects=True, vmem_limit_bytes=64 * 1024 * 1024
        ),
        cost_estimate=pl.CostEstimate(flops=30_000_000, bytes_accessed=1_000_000, transcendentals=32768),
        name="sweeps",
    )(cuts, noise, kappa_sq, pressure_init, source)


def solution(mesh):
    part = P("gx", "gy", "gz")
    return jax.shard_map(
        functools.partial(local, mesh),
        mesh=mesh,
        in_specs=(part, part, P(), part, part),
        out_specs=(part, part),
        check_vma=False,
    )
```

```python
import functools

import jax
import jax.numpy as jnp
from jax import lax
from jax.experimental import pallas as pl
from jax.experimental.pallas import tpu as pltpu
from jax.sharding import PartitionSpec as P

SWEEPS = 8
JACOBI = 8
THETA = 7.125
DELTA = 6.875
LOG_GAIN = 2.0
WIDE = 4
MESH = pl.DeviceIdType.MESH

OFFSETS = [
    (x, y, z)
    for x in (-1, 0, 1)
    for y in (-1, 0, 1)
    for z in (-1, 0, 1)
    if abs(x) + abs(y) + abs(z) >= 1
]
OFFSETS.sort(key=lambda o: (o[2] != 0, abs(o[0]) + abs(o[1]) + abs(o[2]), -abs(o[0])))


def sweep_weights(count):
    ratio_base = THETA / DELTA
    ratio_now = 1.0 / ratio_base
    weights = []
    for index in range(count):
        ratio_next = 1.0 / (2.0 * ratio_base - ratio_now)
        weights.append((ratio_next * ratio_now, 2.0 * ratio_next / DELTA))
        ratio_now = ratio_next
    return weights


class Plan:
    def __init__(self, mesh, cells, flow_rows):
        self.size = (mesh.shape["gx"], mesh.shape["gy"], mesh.shape["gz"])
        self.cells = cells
        self.flow_rows = flow_rows
        self.inset = 3 * cells[0] * self.size[0] // 4
        cx, count = cells[0], self.size[0]
        mean = 3 * cx // 4
        jitter = (mean - 2) // 2
        centre = cx * count // 8
        self.shifts = {}
        for shift in range(1 - count, count):
            low, high = cx, 0
            for tile in range(max(0, -shift), min(count, count - shift)):
                begin = mean * tile + centre - 2 * jitter - cx * (tile + shift)
                end = begin + flow_rows + 2 * jitter
                if max(begin, 0) < min(end, cx):
                    low, high = min(low, max(begin, 0)), max(high, min(end, cx))
            if low < high:
                self.shifts[shift] = (low, high)
        self.shifts[0] = (0, cx)
        self.lowest, self.highest = min(self.shifts), max(self.shifts)
        self.moves = [s for s in sorted(self.shifts, key=abs) if s != 0]
        self.rounds = [(2, 4), (2, 3), (2, 4), (1, 4), (1, 4)]
        self.bases = [sum(n for n, _ in self.rounds[:i]) for i in range(len(self.rounds))]
        self.total = sum(n for n, _ in self.rounds)


def kernel(
    plan,
    cuts_hbm, noise_hbm, kappa_hbm, init_hbm, source_hbm,
    field_ref, pressure_ref,
    dirs, resid, kap, press, coef, charge, perm, maskv,
    init_in, source_in, cuts_in, load_sem,
    send, packed, land_x, land_y, land_xy, land_p,
    move_out, move_in, last, landed,
    send_sem, recv_sem, move_send, move_recv, last_send, last_recv,
):
    cx, cy, cz = plan.cells
    ext_x, ext_y = cx + 2 * WIDE, cy + 8
    me = [lax.axis_index("gx"), lax.axis_index("gy"), lax.axis_index("gz")]
    tiles_y = cy // 8

    def there(offset):
        flag = None
        for at, by, size in zip(me, offset, plan.size):
            if by == 0:
                continue
            one = (at + by < size) if by > 0 else (at + by >= 0)
            flag = one if flag is None else flag & one
        return flag

    def device(offset):
        return tuple(at + by for at, by in zip(me, offset))

    has = {o: there(o) for o in OFFSETS}
    greet = [o for o in OFFSETS] + [(s, 0, 0) for s in plan.moves if abs(s) > 1]
    for s in plan.moves:
        has[(s, 0, 0)] = there((s, 0, 0))
        has[(-s, 0, 0)] = there((-s, 0, 0))

    init_ref, source_ref, cuts_ref = init_in, source_in, cuts_in
    loads = [
        pltpu.make_async_copy(noise_hbm, send.at[0], load_sem.at[0]),
        pltpu.make_async_copy(kappa_hbm, send.at[1], load_sem.at[1]),
        pltpu.make_async_copy(init_hbm, init_in, load_sem.at[2]),
        pltpu.make_async_copy(source_hbm, source_in, load_sem.at[3]),
        pltpu.make_async_copy(cuts_hbm, cuts_in, load_sem.at[4]),
    ]
    for load in loads:
        load.start()

    barrier = pltpu.get_barrier_semaphore()
    expected = jnp.int32(0)
    for o in greet:
        expected = expected + has[o].astype(jnp.int32)

        @pl.when(has[o])
        def _(o=o):
            pl.semaphore_signal(barrier, inc=1, device_id=device(o), device_id_type=MESH)


    dir_l, prs_l = [dirs.at[i] for i in range(4)], [press.at[i] for i in range(4)]
    dir_a, prs_a = dir_l[0], prs_l[0]
    lane = lax.broadcasted_iota(jnp.int32, (8, cz), 1)
    row8 = lax.broadcasted_iota(jnp.int32, (8, cz), 0)

    def offsets_of(width):
        return [(i, o) for i, o in enumerate(OFFSETS) if sum(map(abs, o)) <= width]

    def copies_of(rnd):
        n, w = plan.rounds[rnd]
        listed = [(i, o, 0) for i, o in offsets_of(w)]
        if n > 1:
            extra = [o for o in OFFSETS if o[1] == 0 and o[2] == 0]
            listed = [(len(OFFSETS) + i, o, 1) for i, o in enumerate(extra)] + listed
        return sorted(listed, key=lambda c: (c[1][2] != 0, c[1][0] == 0 or c[1][1] != 0, c[2]))

    def copy_of(rnd, index, o, a):
        n, w = plan.rounds[rnd]
        arrays = pl.ds(plan.bases[rnd], n)
        if o[0] != 0 and o[1] == 0 and o[2] == 0:
            w, arrays = w - a, pl.ds(plan.bases[rnd] + a, 1)
        planes = {0: pl.ds(0, cx), 1: pl.ds(cx - w, w), -1: pl.ds(0, w)}[o[0]]
        rows = {0: pl.ds(0, cy), 1: pl.ds(cy - 8, 8), -1: pl.ds(0, 8)}[o[1]]
        fx, fy = (0 if o[0] > 0 else 1), (0 if o[1] > 0 else 1)
        if o[2] != 0:
            side = 0 if o[2] < 0 else 1
            src = packed.at[side, arrays]
            dst = land_p.at[1 - o[0], 1 - o[1], side, arrays]
        elif o[0] != 0 and o[1] != 0:
            src = send.at[arrays, planes, rows]
            dst = land_xy.at[fx, fy, arrays, pl.ds(0, w)]
        elif o[0] != 0:
            src = send.at[arrays, planes, rows]
            dst = land_x.at[fx, arrays, pl.ds(0, w)]
        else:
            src = send.at[arrays, planes, rows]
            dst = land_y.at[fy, arrays]
        return pltpu.make_async_remote_copy(
            src_ref=src, dst_ref=dst,
            send_sem=send_sem.at[rnd, index], recv_sem=recv_sem.at[rnd, index],
            device_id=device(o), device_id_type=MESH,
        )

    def issue(rnd, chosen):
        for index, o, a in copies_of(rnd):
            if chosen(o):
                @pl.when(has[o])
                def _(index=index, o=o, a=a):
                    copy_of(rnd, index, o, a).start()

    def pack(rnd):
        n, w = plan.rounds[rnd]
        for a in range(n):
            slot = plan.bases[rnd] + a
            low = high = None
            for k in range(cx):
                for j in range(tiles_y):
                    by = (j * cx + k) * w
                    value = send[slot, k, 8 * j : 8 * j + 8]
                    to_low = jnp.where(lane < w, value, 0.0)
                    to_high = jnp.where(lane >= cz - w, value, 0.0)
                    if by:
                        to_low = low + pltpu.roll(to_low, by, 1)
                        to_high = high + pltpu.roll(to_high, cz - by, 1)
                    low, high = to_low, to_high
            packed[0, slot] = low
            packed[1, slot] = high

    def start(rnd, ready=False):
        issue(rnd, lambda o: o[2] == 0)
        if not ready:
            pack(rnd)
        issue(rnd, lambda o: o[2] != 0)

    def finish(rnd, beside):
        for index, o, a in copies_of(rnd):
            if (o[0] == 0) == beside:
                @pl.when(has[tuple(-v for v in o)])
                def _(index=index, o=o, a=a):
                    copy_of(rnd, index, o, a).wait_recv()

    def let_go(rnd):
        for index, o, a in copies_of(rnd):
            @pl.when(has[o])
            def _(index=index, o=o, a=a):
                copy_of(rnd, index, o, a).wait_send()

    def assemble(rnd, a, put, beside, fill=0.0):
        n, w = plan.rounds[rnd]
        slot = plan.bases[rnd] + a
        blank = jnp.full((8, cz), fill, jnp.float32)
        arrived = {}
        for o in OFFSETS:
            if o[2] != 0 and sum(map(abs, o)) <= w and (o[0] == 0) == beside:
                side = 0 if o[2] > 0 else 1
                arrived[o] = jnp.where(has[o], land_p[1 + o[0], 1 + o[1], side, slot], blank)

        def unpack(dx, dy, k, j):
            by = (j * cx + k) * w
            value = blank
            if (dx, dy, 1) in arrived:
                right = pltpu.roll(arrived[dx, dy, 1], (cz - by) % cz, 1)
                value = jnp.where(lane < w, right, value)
                left = pltpu.roll(arrived[dx, dy, -1], by, 1)
                value = jnp.where(lane >= cz - w, left, value)
            return value

        def between(after, before):
            return jnp.where(row8 < w, after, jnp.where(row8 >= 8 - w, before, blank))

        def columns(dx, k, plane):
            for j in range(tiles_y):
                put(1, plane, 8 * j, unpack(dx, 0, k, j))
            put(1, plane, cy, between(unpack(dx, 1, k, 0), unpack(dx, -1, k, tiles_y - 1)))

        for k in range(cx) if beside else ():
            after = jnp.where(has[0, 1, 0], land_y[1, slot, k], blank)
            before = jnp.where(has[0, -1, 0], land_y[0, slot, k], blank)
            put(0, WIDE + k, cy, between(after, before))
            columns(0, k, WIDE + k)
        wide = w - a
        for dx in () if beside else (-1, 1):
            fx = 0 if dx < 0 else 1
            for q in range(wide):
                plane = WIDE - wide + q if dx < 0 else WIDE + cx + q
                k = cx - wide + q if dx < 0 else q
                i = q + a if dx < 0 else q
                big = jnp.where(has[dx, 0, 0], land_x[fx, slot, q], jnp.full((cy, cz), fill, jnp.float32))
                for j in range(tiles_y):
                    put(0, plane, 8 * j, big[8 * j : 8 * j + 8])
                after = jnp.where(has[dx, 1, 0], land_xy[fx, 1, slot, i], blank)
                before = jnp.where(has[dx, -1, 0], land_xy[fx, 0, slot, i], blank)
                put(0, plane, cy, between(after, before))
                columns(dx, k, plane)

    loads[0].wait()
    loads[1].wait()
    pack(0)
    pl.semaphore_wait(barrier, expected)
    start(0, ready=True)
    for load in loads[2:]:
        load.wait()

    inset_begin = cuts_ref[0]
    cut_here = cuts_ref[me[0] + 1]
    count_here = cuts_ref[me[0] + 2] - cut_here

    def pick(ref, shift, r):
        row = cx * (me[0] + shift) + r - inset_begin - cut_here
        value = ref[jnp.clip(row, 0, plan.flow_rows - 1)]
        return jnp.where((row >= 0) & (row < count_here), value, 0.0)

    def move_of(index, shift):
        low, high = plan.shifts[shift]
        return pltpu.make_async_remote_copy(
            src_ref=move_out.at[index, :, pl.ds(low, high - low)],
            dst_ref=move_in.at[index, :, pl.ds(low, high - low)],
            send_sem=move_send.at[index], recv_sem=move_recv.at[index],
            device_id=device((shift, 0, 0)), device_id_type=MESH,
        )

    for index, shift in enumerate(plan.moves):
        low, high = plan.shifts[shift]
        for a, ref in enumerate((init_ref, source_ref)):
            @pl.loop(low, high)
            def _(r, a=a, ref=ref, index=index, shift=shift):
                move_out[index, a, r] = pick(ref, shift, r)

        @pl.when(has[shift, 0, 0])
        def _(index=index, shift=shift):
            move_of(index, shift).start()

    slot_q = plan.bases[2]
    for a, ref in enumerate((init_ref, source_ref)):
        @pl.loop(0, cx)
        def _(r, a=a, ref=ref):
            send[slot_q + a, r] = pick(ref, 0, r)

    row = lax.broadcasted_iota(jnp.int32, (ext_y, cz), 0)
    col = lax.broadcasted_iota(jnp.int32, (ext_y, cz), 1)
    in_rows = (row < cy) | ((row < cy + WIDE) & has[0, 1, 0]) | ((row >= ext_y - WIDE) & has[0, -1, 0])
    in_cols = ((col < WIDE) & has[0, 0, 1]) | ((col >= cz - WIDE) & has[0, 0, -1])
    maskv[0] = jnp.where(in_rows, 1.0, 0.0)
    maskv[1] = jnp.where(in_rows & in_cols, 1.0, 0.0)

    for k in range(cx):
        value = send[0, k]
        resid[0, WIDE + k, 0:cy] = value
        dir_a[0, WIDE + k, 0:cy] = value * (1.0 / THETA)
        field_ref[k] = value * (1.0 / THETA)
        kap[0, WIDE + k, 0:cy] = send[1, k] + 6.0

    first_col, last_col = col == 0, col == cz - 1

    def sides(ref, e):
        core, outer = ref[0, e], ref[1, e]
        core_r, outer_r = pltpu.roll(core, cz - 1, 1), pltpu.roll(outer, cz - 1, 1)
        core_l, outer_l = pltpu.roll(core, 1, 1), pltpu.roll(outer, 1, 1)
        return (
            (core, pltpu.roll(core, 1, 0), pltpu.roll(core, ext_y - 1, 0),
             jnp.where(first_col, outer_l, core_l), jnp.where(last_col, outer_r, core_r)),
            (outer, pltpu.roll(outer, 1, 0), pltpu.roll(outer, ext_y - 1, 0),
             jnp.where(first_col, core_l, outer_l), jnp.where(last_col, core_r, outer_r)),
        )

    weights = sweep_weights(SWEEPS)

    def inside(e):
        at = me[0] * cx - WIDE + e
        return (at >= 0) & (at < plan.size[0] * cx)

    def planes_of(low, high):
        for first, end, own in ((0, WIDE, False), (WIDE, WIDE + cx, True), (WIDE + cx, ext_x, False)):
            first, end = max(first, low), min(end, high)
            if first < end:
                yield first, end, own

    def parts(step, width, beside):
        low, high = WIDE - width + step + 1, WIDE + cx + width - step - 1
        inner_low, inner_high = WIDE + 1 + step, WIDE + cx - 1 - step
        inner_low = min(inner_low, inner_high)
        if beside:
            return [(inner_low, inner_high)]
        return [(low, inner_low), (inner_high, high)]

    def cheb_wide(old, new, weight, low, high):
        for first, end, own in planes_of(low, high):
            @pl.loop(first, end, unroll=2)
            def _(e, own=own):
                okay = jnp.where(inside(e), 1.0, 0.0)
                for zt, (mid, up, down, left, right) in enumerate(sides(old, e)):
                    beside = old[zt, e - 1] + old[zt, e + 1] + (up + down) + (left + right)
                    part = maskv[zt] if own else maskv[zt] * okay
                    rest = resid[zt, e] - (kap[zt, e] * mid - beside) * part
                    resid[zt, e] = rest
                    value = weight[0] * mid + weight[1] * rest
                    new[zt, e] = value
                    if own and zt == 0:
                        field_ref[e - WIDE] = field_ref[e - WIDE] + value[0:cy]

    def cheb_core(old, new, weight, slot, low, high):
        @pl.loop(low, high, unroll=2)
        def _(e):
            k = e - WIDE
            mid, up, down, left, right = sides(old, e)[0]
            beside = old[0, e - 1] + old[0, e + 1] + (up + down) + (left + right)
            rest = (resid[0, e] - (kap[0, e] * mid - beside))[0:cy]
            value = weight[0] * mid[0:cy] + weight[1] * rest
            total = field_ref[k] + value
            field_ref[k] = total
            if slot is None:
                raised = jnp.exp(LOG_GAIN * total)
                send[plan.bases[3], k] = raised
                perm[0, e, 0:cy] = raised
            else:
                resid[0, e, 0:cy] = rest
                new[0, e, 0:cy] = value
                send[slot, k] = value
                send[slot + 1, k] = rest

    def cheb_block(beside, first, count, slot):
        for step in range(count):
            for low, high in parts(step, count, beside):
                if low >= high:
                    continue
                weight = weights[first + step]
                if step < count - 1:
                    cheb_wide(dir_l[step], dir_l[step + 1], weight, low, high)
                else:
                    cheb_core(dir_l[step], dir_a, weight, slot, low, high)

    def put_noise(zt, e, r, value):
        resid[zt, e, r : r + 8] = value
        dir_a[zt, e, r : r + 8] = value * (1.0 / THETA)

    def put_kappa(zt, e, r, value):
        kap[zt, e, r : r + 8] = value + 6.0

    for beside in (True, False):
        finish(0, beside)
        assemble(0, 0, put_noise, beside)
        assemble(0, 1, put_kappa, beside)
        cheb_block(beside, 0, 4, plan.bases[1])
    start(1)

    for index, shift in enumerate(plan.moves):
        low, high = plan.shifts[shift]

        @pl.when(has[-shift, 0, 0])
        def _(index=index, shift=shift, low=low, high=high):
            move_of(index, shift).wait_recv()
            for a in range(2):
                send[slot_q + a, low:high] = send[slot_q + a, low:high] + move_in[index, a, low:high]

        @pl.when(has[shift, 0, 0])
        def _(index=index, shift=shift):
            move_of(index, shift).wait_send()

    start(2)

    def put_dir(zt, e, r, value):
        dir_a[zt, e, r : r + 8] = value

    def put_resid(zt, e, r, value):
        resid[zt, e, r : r + 8] = value

    for beside in (True, False):
        finish(1, beside)
        assemble(1, 0, put_dir, beside)
        assemble(1, 1, put_resid, beside)
        cheb_block(beside, 4, 3, None)
    start(3)


    def put_init(zt, e, r, value):
        prs_a[zt, e, r : r + 8] = value

    def put_charge(zt, e, r, value):
        charge[zt, e, r : r + 8] = value

    for beside in (True, False):
        finish(2, beside)
        assemble(2, 0, put_init, beside)
        assemble(2, 1, put_charge, beside)
    for k in range(cx):
        prs_a[0, WIDE + k, 0:cy] = send[slot_q, k]
        charge[0, WIDE + k, 0:cy] = send[slot_q + 1, k]


    def put_perm(zt, e, r, value):
        perm[zt, e, r : r + 8] = value


    top = (row == 0) & (me[1] == 0)
    bottom = (row == cy - 1) & (me[1] == plan.size[1] - 1)
    near = first_col & (me[2] == 0)
    far = last_col & (me[2] == plan.size[2] - 1)

    def harmonic(own, other):
        return 2.0 * own * other / (own + other)

    def couple_x(e):
        plane = me[0] * cx - WIDE + e - inset_begin
        pair = (plane >= 0) & (plane < plan.inset - 1)
        for zt in range(2):
            coef[0, zt, e] = jnp.where(pair, harmonic(perm[zt, e], perm[zt, e + 1]), 0.0)

    def couple(e):
        plane = me[0] * cx - WIDE + e - inset_begin
        okay = (plane >= 0) & (plane < plan.inset)
        (core, _, core_down, _, core_right), (outer, _, outer_down, _, outer_right) = sides(perm, e)
        core_z = jnp.where(okay, harmonic(core, core_right), 0.0)
        outer_z = jnp.where(okay, harmonic(outer, outer_right), 0.0)
        core_back, outer_back = pltpu.roll(core_z, 1, 1), pltpu.roll(outer_z, 1, 1)
        core_left = jnp.where(first_col, outer_back, core_back)
        outer_left = jnp.where(first_col, core_back, outer_back)
        core_left, core_fore = jnp.where(near, core, core_left), jnp.where(far, core, core_z)
        for zt, mid, down, z_left, z_right, z_pair in (
            (0, core, core_down, core_left, core_fore, core_z),
            (1, outer, outer_down, outer_left, outer_z, outer_z),
        ):
            below = jnp.where(plane == 0, mid, coef[0, zt, e - 1])
            above = jnp.where(plane == plan.inset - 1, mid, coef[0, zt, e])
            y_pair = jnp.where(okay, harmonic(mid, down), 0.0)
            y_up = jnp.where(top, mid, pltpu.roll(y_pair, 1, 0))
            y_down = jnp.where(bottom, mid, y_pair)
            total = below + above + y_up + y_down + z_left + z_right
            valid = (maskv[zt] > 0.5) & okay
            coef[1, zt, e] = y_pair
            coef[2, zt, e] = z_pair
            coef[3, zt, e] = jnp.where(valid, 1.0 / total, 0.0)

    def flux(old, e, outer_too):
        core, outer = old[0, e], old[1, e]
        core_z, outer_z = coef[2, 0, e], coef[2, 1, e]
        core_r, outer_r = pltpu.roll(core, cz - 1, 1), pltpu.roll(outer, cz - 1, 1)
        core_l, outer_l = pltpu.roll(core * core_z, 1, 1), pltpu.roll(outer * outer_z, 1, 1)
        along = [jnp.where(last_col, outer_r, core_r) * core_z + jnp.where(first_col, outer_l, core_l)]
        if outer_too:
            along.append(jnp.where(last_col, core_r, outer_r) * outer_z + jnp.where(first_col, core_l, outer_l))
        values = []
        for zt, value in enumerate(along):
            mid, y_pair = (core, outer)[zt], coef[1, zt, e]
            value = value + charge[zt, e]
            value = value + (coef[0, zt, e - 1] * old[zt, e - 1] + coef[0, zt, e] * old[zt, e + 1])
            value = value + (y_pair * pltpu.roll(mid, ext_y - 1, 0) + pltpu.roll(y_pair * mid, 1, 0))
            values.append(value * coef[3, zt, e])
        return values

    def jacobi_wide(old, new, low, high):
        @pl.loop(low, high, unroll=2)
        def _(e):
            for zt, value in enumerate(flux(old, e, True)):
                new[zt, e] = value

    def jacobi_core(old, new, slot, low, high):
        @pl.loop(low, high, unroll=2)
        def _(e):
            k = e - WIDE
            value = flux(old, e, False)[0][0:cy]
            if slot is None:
                last[k] = value
            else:
                new[0, e, 0:cy] = value
                send[slot, k] = value

    def jacobi_block(beside, count, slot):
        for step in range(count):
            for low, high in parts(step, count, beside):
                if low >= high:
                    continue
                if step < count - 1:
                    jacobi_wide(prs_l[step], prs_l[step + 1], low, high)
                else:
                    jacobi_core(prs_l[step], prs_a, slot, low, high)

    def over(ranges, body):
        for low, high in ranges:
            pl.loop(low, high, unroll=2)(body)

    inner, end = WIDE + cx - 1, ext_x - 1
    for beside in (True, False):
        finish(3, beside)
        assemble(3, 0, put_perm, beside, fill=1.0)
        over([(WIDE, inner)] if beside else [(0, WIDE), (inner, end)], couple_x)
        over([(WIDE + 1, inner)] if beside else [(1, WIDE + 1), (inner, end)], couple)
        jacobi_block(beside, 4, plan.bases[4])
    start(4)
    for beside in (True, False):
        finish(4, beside)
        assemble(4, 0, put_init, beside)
        jacobi_block(beside, 4, None)

    def last_of(index, shift):
        low, high = plan.shifts[shift]
        at = (shift - plan.lowest) * cx + low
        return pltpu.make_async_remote_copy(
            src_ref=last.at[pl.ds(low, high - low)],
            dst_ref=landed.at[pl.ds(at, high - low)],
            send_sem=last_send.at[index], recv_sem=last_recv.at[index],
            device_id=device((-shift, 0, 0)), device_id_type=MESH,
        )

    for index, shift in enumerate(plan.moves):
        @pl.when(has[-shift, 0, 0])
        def _(index=index, shift=shift):
            last_of(index, shift).start()

    landed[-plan.lowest * cx : (1 - plan.lowest) * cx] = last[...]
    for index, shift in enumerate(plan.moves):
        @pl.when(has[shift, 0, 0])
        def _(index=index, shift=shift):
            last_of(index, shift).wait_recv()

    window = (plan.highest - plan.lowest + 1) * cx

    @pl.loop(0, plan.flow_rows)
    def _(j):
        at = inset_begin + cut_here + j - cx * (me[0] + plan.lowest)
        value = landed[jnp.clip(at, 0, window - 1)]
        pressure_ref[j] = jnp.where(j < count_here, value, 0.0)

    for index, shift in enumerate(plan.moves):
        @pl.when(has[-shift, 0, 0])
        def _(index=index, shift=shift):
            last_of(index, shift).wait_send()

    for rnd in range(len(plan.rounds)):
        let_go(rnd)


def local(mesh, noise, kappa_sq, cuts, pressure_init, source):
    cells, flow_rows = noise.shape, pressure_init.shape[0]
    plan = Plan(mesh, cells, flow_rows)
    cx, cy, cz = cells
    block = (2, cx + 2 * WIDE, cy + 8, cz)
    moves = max(1, len(plan.moves))
    f32 = jnp.float32
    vmem = lambda *shape: pltpu.VMEM(shape, f32)
    sems = lambda *shape: pltpu.SemaphoreType.DMA(shape)
    total = plan.total
    return pl.pallas_call(
        functools.partial(kernel, plan),
        out_shape=(
            jax.ShapeDtypeStruct(noise.shape, f32),
            jax.ShapeDtypeStruct(pressure_init.shape, f32),
        ),
        in_specs=[pl.BlockSpec(memory_space=pl.ANY)] * 5,
        out_specs=(pl.BlockSpec(memory_space=pltpu.VMEM),) * 2,
        scratch_shapes=[
            vmem(4, *block), vmem(*block), vmem(*block), vmem(4, *block),
            vmem(4, *block), vmem(*block), vmem(*block), vmem(2, cy + 8, cz),
            vmem(*pressure_init.shape), vmem(*source.shape),
            pltpu.SMEM(cuts.shape, jnp.int32), sems(5),
            vmem(total, cx, cy, cz), vmem(2, total, 8, cz),
            vmem(2, total, WIDE, cy, cz), vmem(2, total, cx, 8, cz),
            vmem(2, 2, total, WIDE, 8, cz), vmem(3, 3, 2, total, 8, cz),
            vmem(moves, 2, cx, cy, cz), vmem(moves, 2, cx, cy, cz),
            vmem(cx, cy, cz), vmem((plan.highest - plan.lowest + 1) * cx, cy, cz),
            sems(len(plan.rounds), len(OFFSETS) + 2), sems(len(plan.rounds), len(OFFSETS) + 2),
            sems(moves), sems(moves), sems(moves), sems(moves),
        ],
        compiler_params=pltpu.CompilerParams(
            collective_id=0, has_side_effects=True, vmem_limit_bytes=64 * 1024 * 1024
        ),
        cost_estimate=pl.CostEstimate(flops=30_000_000, bytes_accessed=1_000_000, transcendentals=32768),
        name="sweeps",
    )(cuts, noise, kappa_sq, pressure_init, source)


def solution(mesh):
    part = P("gx", "gy", "gz")
    return jax.shard_map(
        functools.partial(local, mesh),
        mesh=mesh,
        in_specs=(part, part, P(), part, part),
        out_specs=(part, part),
        check_vma=False,
    )
```
